32 devices in a mesh: dp: 16 (over z, y, core), tensor: 2 (over x).
Axes of the slice: x: 2, y: 2, z: 4, core: 2. Of those that a mesh axis runs over, the one named last changes fastest.
Arguments:
- tokens: bfloat16 [8192, 2048], P(('dp', 'tensor')), may hold values from -6 to 6
- segments: int32 [16, 512], P('dp'), may hold values from 0 to 7, never falling along the last dimension, each value on 1 to 256 neighbouring positions
- gain_attn: bfloat16 [2048], P('dp'), may hold values from 0.5 to 1.5
- gain_ffn: bfloat16 [2048], P('dp'), may hold values from 0.5 to 1.5
- w_query: bfloat16 [2048, 2048], P('dp', 'tensor'), may hold values from -0.125 to 0.125
- w_key: bfloat16 [2048, 2048], P('dp', 'tensor'), may hold values from -0.125 to 0.125
- w_value: bfloat16 [2048, 2048], P('dp', 'tensor'), may hold values from -0.125 to 0.125
- w_out: bfloat16 [2048, 2048], P('dp', 'tensor'), may hold values from -3 to 3
- w_gate: bfloat16 [2048, 8192], P('dp', 'tensor'), may hold values from -0.125 to 0.125
- w_up: bfloat16 [2048, 8192], P('dp', 'tensor'), may hold values from -0.125 to 0.125
- w_down: bfloat16 [2048, 8192], P('dp', 'tensor'), may hold values from -0.0625 to 0.0625
- cotangent: bfloat16 [8192, 2048], P(('dp', 'tensor')), may hold values from -6 to 6
Outputs:
- output: bfloat16 [8192, 2048], P(('dp', 'tensor'))
- grad_tokens: float32 [8192, 2048], P(('dp', 'tensor'))
- grad_gain_attn: float32 [2048], P('dp')
- grad_gain_ffn: float32 [2048], P('dp')
- grad_query: float32 [2048, 2048], P('dp', 'tensor')
- grad_key: float32 [2048, 2048], P('dp', 'tensor')
- grad_value: float32 [2048, 2048], P('dp', 'tensor')
- grad_out: float32 [2048, 2048], P('dp', 'tensor')
- grad_gate: float32 [2048, 8192], P('dp', 'tensor')
- grad_up: float32 [2048, 8192], P('dp', 'tensor')
- grad_down: float32 [2048, 8192], P('dp', 'tensor')
The draws below stay inside these ranges and needn't reach their ends.
Inputs may be any that keep to these rules, and one draw needn't show every extreme that they name: `segments`: in each row, document numbers never fall; a document holds 1 to 256 tokens, and some document holds exactly 256.
All inputs are finite; a program needn't handle non-finite values.
Results may differ from the reference program's by a relative error of at most 0.014.
Values may be sent and summed in bfloat16 or wider, within the bound.
No kernel may reach another device: no remote copies, remote signals or barrier semaphores. Data moves between devices by JAX's collectives and lax.ppermute only.
A program may use at most 320 MiB of HBM per device.

```python
import math
import jax
import jax.numpy as jnp
import numpy as np
from jax import lax

D = 2048
HEADS = 16
HEAD_DIM = 128
FF = 8192
SEQ_LEN = 512
DOCS = 8
NSEQ = 16
TOKENS = 8192


def spiked(values, own_key, source, target, parts, factor):
    owner, partner = [(jnp.arange(values.shape[dim]) // (values.shape[dim] // parts)).reshape([-1 if axis == dim else 1 for axis in range(values.ndim)]) for dim in (source, target)]
    chosen = jax.random.permutation(own_key, parts)[partner]
    strong = (owner == chosen) | (owner == (partner + parts // 2) % parts)
    return jnp.where(strong, factor * values, values)


def shard_levels(rng, extent, cuts, least, largest):
    def one(dim, blocks):
        steps = jax.random.uniform(jax.random.fold_in(jax.random.fold_in(rng, 6), dim), (blocks,), jnp.float32, least / len(cuts), largest / len(cuts))
        return jnp.repeat(jnp.exp(steps), extent[dim] // blocks).reshape((-1,) + (1,) * (len(extent) - dim - 1))

    level = one(*cuts[0])
    for cut in cuts[1:]:
        level = level * one(*cut)
    return level


def profile(count, total, bound, skew):
    weights = [(1 << 20) // math.isqrt(grade ** skew) + 1 for grade in range(2, count + 1)]
    surplus, holding = total - bound - (count - 1), [1] * (count - 1)
    while surplus > 0:
        free = [i for i in range(count - 1) if holding[i] < bound]
        pool, left = sum([weights[i] for i in free]), surplus
        for i in free:
            more = min(bound - holding[i], max(1, left * weights[i] // pool), surplus)
            holding[i] = holding[i] + more
            surplus = surplus - more
    return np.array([bound] + holding)


def ragged(stream_key, number_of, total, limit, lean):
    if number_of == 2:
        one = jax.random.randint(stream_key, (), max(1, total - limit), min(limit, total - 1) + 1)
        return jnp.stack([one, total - one])
    tallies = jnp.asarray(profile(number_of, total, limit, lean), jnp.int32)
    pairs = (number_of - 1) // 2
    giver, sink = tallies[1:1 + 2 * pairs:2], tallies[2:2 + 2 * pairs:2]
    slack = jnp.minimum(giver - 1, limit - sink)
    passed = jax.random.randint(jax.random.fold_in(stream_key, 1), (pairs,), 0, 1 << 20) % (slack + 1)
    tallies = tallies.at[1:1 + 2 * pairs:2].set(giver - passed).at[2:2 + 2 * pairs:2].set(sink + passed)
    return tallies[jax.random.permutation(jax.random.fold_in(stream_key, 2), number_of)]


def bell_draw(own_key, extent, width, bound, shards=(), kind=jnp.bfloat16):
    values = width * jax.random.normal(own_key, extent, jnp.float32)
    if shards:
        values = values * shard_levels(own_key, extent, shards, -0.22, 0.18)
    return jnp.clip(values, -bound, bound).astype(kind)


def bell_draw_with(own_key, dims, width, bound, cuts, heavy, held_as=jnp.bfloat16):
    entries = width * jax.random.normal(own_key, dims, jnp.float32)
    if cuts:
        entries = entries * shard_levels(own_key, dims, cuts, -0.22, 0.18)
    return jnp.clip(spiked(entries, jax.random.fold_in(own_key, 3), *heavy), -bound, bound).astype(held_as)


def setup_inputs(seed: int = 0) -> dict:
    streams_of = jax.random.split(jax.random.key(seed), 13)
    tokens = bell_draw_with(streams_of[0], (TOKENS, D), 1.0, 6.0, ((0, 32),), (0, 1, 32, 2.75))
    segments = jax.vmap(lambda own: jnp.searchsorted(jnp.cumsum(ragged(own, DOCS, SEQ_LEN, SEQ_LEN // 2, 2)), jnp.arange(SEQ_LEN), side="right"))(jax.random.split(streams_of[1], NSEQ)).reshape((NSEQ, SEQ_LEN)).astype(jnp.int32)
    gain_attn = jnp.clip(1.0 + 0.1 * jax.random.normal(streams_of[2], (D,), jnp.float32), 0.5, 1.5).astype(jnp.bfloat16)
    gain_ffn = jnp.clip(1.0 + 0.1 * jax.random.normal(streams_of[3], (D,), jnp.float32), 0.5, 1.5).astype(jnp.bfloat16)
    w_query = bell_draw(streams_of[4], (D, D), D ** -0.5, 0.125, ((0, 16), (1, 2)))
    w_key = bell_draw(streams_of[5], (D, D), D ** -0.5, 0.125, ((0, 16), (1, 2)))
    w_value = bell_draw(streams_of[6], (D, D), D ** -0.5, 0.125, ((0, 16), (1, 2)))
    w_out = bell_draw(streams_of[7], (D, D), (max(D // 512, 2)) ** -0.5, 3.0, ((0, 16), (1, 2)))
    w_gate = bell_draw(streams_of[8], (D, FF), D ** -0.5, 0.125, ((0, 16), (1, 2)))
    w_up = bell_draw(streams_of[9], (D, FF), D ** -0.5, 0.125, ((0, 16), (1, 2)))
    w_down = bell_draw(streams_of[10], (D, FF), FF ** -0.5, 0.0625, ((0, 16), (1, 2)))
    cotangent = bell_draw_with(streams_of[11], (TOKENS, D), 1.0, 6.0, ((0, 32),), (0, 1, 32, 2.75))
    return {"tokens": tokens, "segments": segments, "gain_attn": gain_attn, "gain_ffn": gain_ffn, "w_query": w_query, "w_key": w_key, "w_value": w_value, "w_out": w_out, "w_gate": w_gate, "w_up": w_up, "w_down": w_down, "cotangent": cotangent}


@jax.custom_vjp
def low(v):
    return lax.optimization_barrier(v.astype(jnp.bfloat16)).astype(jnp.float32)

@jax.custom_vjp
def low_back(v):
    return v

def low_keep(v):
    return (low(v), None)

def low_pass(kept, grad):
    return (grad,)

def back_keep(v):
    return (v, None)

def back_low(kept, grad):
    return (low(grad),)
low.defvjp(low_keep, low_pass)
low_back.defvjp(back_keep, back_low)
epsilon = 1e-05
theta = 10000.0
highest = lax.Precision.HIGHEST

def positions_of(segment_row):
    length = segment_row.shape[-1]
    places = jnp.arange(length, dtype=jnp.int32)
    starts = jnp.concatenate([jnp.ones((1,), jnp.bool_), segment_row[1:] != segment_row[:-1]])
    begins = lax.cummax(jnp.where(starts, places, 0).astype(jnp.int32), axis=0)
    return places - begins

def rotary_tables(positions, half):
    freqs = theta ** (-(jnp.arange(half, dtype=jnp.float32) * 2.0 / (2 * half)))
    angles = positions.astype(jnp.float32)[..., None] * freqs
    return (jnp.cos(angles), jnp.sin(angles))

def rotate(values, cosine, sine):
    half = values.shape[-1] // 2
    first = values[..., :half]
    second = values[..., half:]
    cosine = cosine[..., None, :]
    sine = sine[..., None, :]
    return jnp.concatenate([first * cosine - second * sine, second * cosine + first * sine], axis=-1)

def normalize(rows, gain):
    scale = lax.rsqrt(lax.optimization_barrier(jnp.mean(rows * rows, axis=-1, keepdims=True)) + epsilon)
    return rows * scale * gain

def matmul(left, right):
    return jnp.dot(left, right, precision=highest, preferred_element_type=jnp.float32)

def attend(block):
    queries, keys_rot, values, segment_row = block
    length = queries.shape[0]
    places = jnp.arange(length, dtype=jnp.int32)
    live = (segment_row[:, None] == segment_row[None, :]) & (places[None, :] <= places[:, None])
    dots = low_back(jnp.einsum('qhd,khd->hqk', queries, keys_rot, precision=highest) * (1.0 / math.sqrt(HEAD_DIM)))
    weights = low(jnp.where(live[None], jax.nn.sigmoid(dots - math.log(SEQ_LEN)), 0.0))
    return jnp.einsum('hqk,khd->qhd', weights, values, precision=highest)

def layer(inputs, segs, gain_one, gain_two, w_query, w_key, w_value, w_out, w_gate, w_up, w_down):
    count = segs.shape[0]
    normed_one = low(normalize(inputs, gain_one))
    positions = jax.vmap(positions_of)(segs)
    cosine, sine = rotary_tables(positions, HEAD_DIM // 2)
    shape = (count, SEQ_LEN, HEADS, HEAD_DIM)
    queries = low(rotate(low_back(matmul(normed_one, w_query)).reshape(shape), cosine, sine))
    keys_rot = low(rotate(low_back(matmul(normed_one, w_key)).reshape(shape), cosine, sine))
    values = low(low_back(matmul(normed_one, w_value))).reshape(shape)
    mixed = lax.map(jax.checkpoint(attend), (queries, keys_rot, values, segs))
    mixed = low(low_back(mixed.reshape(count * SEQ_LEN, D)))
    middle = inputs + low_back(matmul(mixed, w_out.T))
    normed_two = low(normalize(middle, gain_two))
    gate = low_back(matmul(normed_two, w_gate))
    upward = low_back(matmul(normed_two, w_up))
    hidden = low(jax.nn.silu(gate) * upward)
    return middle + matmul(hidden, w_down.T)

def reference(tokens, segments, gain_attn, gain_ffn, w_query, w_key, w_value, w_out, w_gate, w_up, w_down, cotangent):
    group = math.gcd(NSEQ, max(1, 4096 // SEQ_LEN))
    params = tuple((item.astype(jnp.float32) for item in (gain_attn, gain_ffn, w_query, w_key, w_value, w_out, w_gate, w_up, w_down)))
    inputs = tokens.astype(jnp.float32).reshape(NSEQ // group, group * SEQ_LEN, D)
    grads_in = cotangent.astype(jnp.float32).reshape(NSEQ // group, group * SEQ_LEN, D)
    seg_groups = segments.reshape(NSEQ // group, group, SEQ_LEN)

    def step(totals, block):
        rows, grad_rows, segs = block
        result, pullback = jax.vjp(lambda first, *rest: layer(first, segs, *rest), rows, *params)
        grads = pullback(grad_rows)
        return (tuple((total + grad for total, grad in zip(totals, grads[1:]))), (result, grads[0]))
    zeros = tuple((jnp.zeros(item.shape, jnp.float32) for item in params))
    totals, (results, grad_inputs) = lax.scan(step, zeros, (inputs, grads_in, seg_groups))
    return (results.reshape(TOKENS, D).astype(jnp.bfloat16), grad_inputs.reshape(TOKENS, D), totals[0], totals[1], totals[2], totals[3], totals[4], totals[5], totals[6], totals[7], totals[8])
```

```python
import math

import jax
import jax.numpy as jnp
from jax import lax
from jax.sharding import PartitionSpec as P

HEAD_DIM = 128
SEQ_LEN = 512
PLANE = 4
CHUNKS = 4

epsilon = 1e-05
theta = 10000.0
low = jnp.bfloat16
f32 = jnp.float32


def dot(left, right):
    return jnp.dot(left, right, preferred_element_type=f32)


def dot_rt(left, right):
    return lax.dot_general(left, right, (((1,), (1,)), ((), ())), preferred_element_type=f32)


def dot_lt(left, right):
    return lax.dot_general(left, right, (((0,), (0,)), ((), ())), preferred_element_type=f32)


def after(value, *earlier):
    return lax.optimization_barrier((value,) + earlier)[0]


def swap_x(value):
    return lax.ppermute(value, "tensor", [(0, 1), (1, 0)])


def swap_dp(value, flip):
    count = lax.axis_size("dp")
    return lax.ppermute(value, "dp", [(i, i ^ flip) for i in range(count)])


def swap_c(value):
    return swap_dp(value, 1)


def swap_y(value):
    return swap_dp(value, 2)


def line_shift(value, planes, way):
    pairs = []
    for p in planes:
        pairs += [(p * PLANE + j, (p + way) * PLANE + j) for j in range(PLANE)]
    return lax.ppermute(value, "dp", pairs)


def gather_plane(own):
    half = own.shape[0] // 2
    from_c = swap_c(own)
    from_x = swap_x(own)
    from_y = swap_y(own)
    from_xy = jnp.concatenate([swap_y(from_x[:half]), swap_x(from_y[half:])], axis=0)
    from_cx = swap_c(from_x)
    from_cy = swap_c(from_y)
    from_cxy = swap_c(from_xy)
    return jnp.concatenate(
        [own, from_x, from_c, from_cx, from_y, from_xy, from_cy, from_cxy], axis=0
    )


def scatter_plane(partial):
    rows = partial.shape[0] // 8
    half = rows // 2
    width = partial.shape[1]
    blocks = partial.reshape(2, 2, 2, rows, width)
    other = swap_c(blocks[:, 1].astype(low))
    both = blocks[:, 0].astype(f32) + other.astype(f32)
    top, bottom = both[:, :, :half], both[:, :, half:]
    top_x = swap_x(top[:, 1].astype(low))
    bottom_y = swap_y(bottom[1].astype(low))
    top = top[:, 0] + top_x.astype(f32)
    bottom = bottom[0] + bottom_y.astype(f32)
    top_y = swap_y(top[1].astype(low))
    bottom_x = swap_x(bottom[1].astype(low))
    return jnp.concatenate([top[0] + top_y.astype(f32), bottom[0] + bottom_x.astype(f32)], axis=0)


def to_columns(parts, place):
    rows, _, width = parts.shape
    result = jnp.zeros((PLANE, rows, width), parts.dtype)
    for flip in range(PLANE):
        piece = lax.dynamic_index_in_dim(parts, place ^ flip, 1, keepdims=False)
        if flip:
            piece = swap_dp(piece, flip)
        result = lax.dynamic_update_index_in_dim(result, piece, place ^ flip, 0)
    return result.reshape(PLANE * rows, width)


def to_rows(block, place):
    width = block.shape[1]
    parts = block.reshape(PLANE, block.shape[0] // PLANE, width)
    result = jnp.zeros((parts.shape[1], PLANE, width), parts.dtype)
    for flip in range(PLANE):
        piece = lax.dynamic_index_in_dim(parts, place ^ flip, 0, keepdims=False)
        if flip:
            piece = swap_dp(piece, flip)
        result = lax.dynamic_update_index_in_dim(result, piece, place ^ flip, 1)
    return result


def gather_line(own, depth, level, count):
    up, down = own, own
    ups, downs = [], []
    for step in range(1, count):
        up = line_shift(up, range(step - 1, count - 1), 1)
        down = line_shift(down, range(1, count + 1 - step), -1)
        ups.append(up)
        downs.append(down)
    result = jnp.zeros((count,) + own.shape, own.dtype)
    result = lax.dynamic_update_index_in_dim(result, own, level, 0)
    for step in range(1, count):
        piece = jnp.where(level >= step, ups[step - 1], downs[count - step - 1])
        result = lax.dynamic_update_index_in_dim(
            result, piece, lax.rem(level - step + count, count), 0
        )
    mark = (ups[max(count - 3, 0)], downs[max(count - 3, 0)]) if count > 1 else (own,)
    return result.reshape((count * own.shape[0],) + own.shape[1:]), mark


def scatter_line(blocks, level, count, wait):
    if count == 1:
        return blocks[0].astype(f32), ()
    got_up = got_down = None
    ups = []
    for step in range(1, count):
        send_up = lax.dynamic_index_in_dim(
            blocks, lax.rem(level - step + count, count), 0, keepdims=False
        )
        send_down = lax.dynamic_index_in_dim(
            blocks, lax.rem(level + step, count), 0, keepdims=False
        )
        if got_up is None:
            send_up, send_down = send_up.astype(low), send_down.astype(low)
            if wait:
                send_up = after(send_up, *wait)
                send_down = after(send_down, *wait)
        else:
            send_up = (send_up.astype(f32) + got_up.astype(f32)).astype(low)
            send_down = (send_down.astype(f32) + got_down.astype(f32)).astype(low)
        got_up = line_shift(send_up, range(0, min(step, count - 1)), 1)
        got_down = line_shift(send_down, range(max(count - step, 1), count), -1)
        ups.append((got_up, got_down))
    own = lax.dynamic_index_in_dim(blocks, level, 0, keepdims=False)
    total = own.astype(f32) + got_up.astype(f32) + got_down.astype(f32)
    return total, ups[max(count - 3, 0)]


def normalize(rows):
    scale = lax.rsqrt(jnp.mean(rows * rows, axis=-1, keepdims=True) + epsilon)
    return rows * scale, scale


def norm_back(grad_normed, unit_rows, scale, gain):
    inner = grad_normed * gain
    mean_term = jnp.mean(inner * unit_rows, axis=-1, keepdims=True)
    return scale * (inner - unit_rows * mean_term), jnp.sum(grad_normed * unit_rows, axis=0)


def rotate(values, cosine, sine):
    half = values.shape[-1] // 2
    first, second = values[..., :half], values[..., half:]
    return jnp.concatenate(
        [first * cosine - second * sine, second * cosine + first * sine], axis=-1
    )


def unrotate(values, cosine, sine):
    half = values.shape[-1] // 2
    first, second = values[..., :half], values[..., half:]
    return jnp.concatenate(
        [first * cosine + second * sine, second * cosine - first * sine], axis=-1
    )


def gather_gains(gains, place, level, count):
    plane = jnp.zeros((PLANE,) + gains.shape, gains.dtype)
    for flip in range(PLANE):
        piece = swap_dp(gains, flip) if flip else gains
        plane = lax.dynamic_update_index_in_dim(plane, piece, place ^ flip, 0)
    whole = jnp.zeros((count,) + plane.shape, gains.dtype)
    whole = lax.dynamic_update_index_in_dim(whole, plane, level, 0)
    total = count * PLANE
    for step in range(1, count):
        pairs = [(i, (i + step * PLANE) % total) for i in range(total)]
        piece = lax.ppermute(plane, "dp", pairs)
        whole = lax.dynamic_update_index_in_dim(
            whole, piece, lax.rem(level - step + count, count), 0
        )
    return jnp.moveaxis(whole, 2, 0).reshape(gains.shape[0], -1)


def scatter_gain(part, place, level, count):
    part = part + swap_x(part)
    blocks = part.reshape(count, PLANE, -1)
    mine = lax.dynamic_index_in_dim(blocks, place, 1, keepdims=False)
    for flip in range(1, PLANE):
        mine = mine + swap_dp(
            lax.dynamic_index_in_dim(blocks, place ^ flip, 1, keepdims=False), flip
        )
    result = lax.dynamic_index_in_dim(mine, level, 0, keepdims=False)
    total = count * PLANE
    for step in range(1, count):
        pairs = [(i, (i + step * PLANE) % total) for i in range(total)]
        result = result + lax.ppermute(
            lax.dynamic_index_in_dim(mine, lax.rem(level + step, count), 0, keepdims=False),
            "dp",
            pairs,
        )
    return result


def local(
    tokens,
    segments,
    gain_attn,
    gain_ffn,
    w_query,
    w_key,
    w_value,
    w_out,
    w_gate,
    w_up,
    w_down,
    cotangent,
):
    seq_len = segments.shape[1]
    shard = w_query.shape[0]
    model = tokens.shape[1]
    count = lax.axis_size("dp") // PLANE
    me = lax.axis_index("dp")
    side = lax.axis_index("tensor")
    level, place = me // PLANE, lax.rem(me, PLANE)
    scale_dot = 1.0 / math.sqrt(HEAD_DIM)
    shift = -math.log(SEQ_LEN)
    width = w_query.shape[1] // PLANE
    heads = width // HEAD_DIM
    units = w_gate.shape[1] // PLANE
    chunk = units // CHUNKS

    attn_parts = jnp.concatenate(
        [w.reshape(shard, PLANE, width) for w in (w_query, w_key, w_value, w_out)], axis=2
    )
    attn_block = to_columns(attn_parts, place)
    attn_weights, mark = gather_line(attn_block, shard, level, count)
    w_qkv, w_o = attn_weights[:, : 3 * width], attn_weights[:, 3 * width :]
    chunk_weights = []
    wide = [w.reshape(shard, PLANE, units) for w in (w_gate, w_up, w_down)]
    for k in range(CHUNKS):
        parts = jnp.concatenate([w[:, :, k * chunk : (k + 1) * chunk] for w in wide], axis=2)
        block = after(to_columns(parts, place), *mark)
        gathered, mark = gather_line(block, shard, level, count)
        chunk_weights.append(gathered)

    gains = gather_gains(jnp.stack([gain_attn, gain_ffn]), place, level, count).astype(f32)
    gain_first, gain_second = gains[0], gains[1]
    inputs = tokens.astype(f32)
    unit_one, scale_one = normalize(inputs)
    rows_one = gather_plane((unit_one * gain_first).astype(low))
    grad_rows = gather_plane(after(cotangent, rows_one))
    seg = jnp.concatenate([segments] + [swap_dp(segments, flip) for flip in range(1, PLANE)], axis=0)
    places = lax.rem(jnp.arange(seq_len, dtype=jnp.int32) + side * (seq_len // 2), seq_len)
    seg = jnp.where(side == 0, seg, jnp.roll(seg, seq_len // 2, axis=1))
    same = seg[:, :, None] == seg[:, None, :]
    live = same & (places[None, None, :] <= places[None, :, None])
    positions = jnp.sum(live.astype(jnp.int32), axis=2) - 1
    freqs = theta ** (-(jnp.arange(HEAD_DIM // 2, dtype=f32) * 2.0 / HEAD_DIM))
    angles = positions.astype(f32)[..., None] * freqs
    cosine, sine = jnp.cos(angles)[:, :, None, :], jnp.sin(angles)[:, :, None, :]

    qkv = dot(rows_one, w_qkv).reshape(PLANE, seq_len, 3, heads, HEAD_DIM)
    queries = rotate(qkv[:, :, 0], cosine, sine).astype(low)
    keys = rotate(qkv[:, :, 1], cosine, sine).astype(low)
    values = qkv[:, :, 2].astype(low)

    def weights():
        dots = (
            jnp.einsum("nqhd,nkhd->nhqk", queries, keys, preferred_element_type=f32) * scale_dot
        )
        return jnp.where(live[:, None], jax.nn.sigmoid(dots + shift), 0.0)

    probs = weights()
    probs_low = probs.astype(low)
    mixed = jnp.einsum("nhqk,nkhd->nqhd", probs_low, values, preferred_element_type=f32)
    mixed = mixed.reshape(PLANE * seq_len, width).astype(low)
    middle = inputs + scatter_plane(dot_rt(mixed, w_o))
    unit_two, scale_two = normalize(middle)
    rows_two = gather_plane((unit_two * gain_second).astype(low))

    hiddens, grad_acts, ffn_grads = [], [], []
    wait = ()
    for k in range(CHUNKS):
        part = chunk_weights[k]
        wg, wu, wd = part[:, :chunk], part[:, chunk : 2 * chunk], part[:, 2 * chunk :]
        gate = dot(rows_two, wg)
        upward = dot(rows_two, wu)
        grad_hidden = dot(grad_rows, wd)
        gate_sig = jax.nn.sigmoid(gate)
        silu = gate * gate_sig
        hidden = (silu * upward).astype(low)
        grad_gate = (grad_hidden * upward * gate_sig * (1.0 + gate * (1.0 - gate_sig))).astype(low)
        grad_up = (grad_hidden * silu).astype(low)
        hiddens.append(hidden)
        grad_acts.append((grad_gate, grad_up))
        grads = jnp.concatenate(
            [
                dot_lt(rows_two, grad_gate).astype(low),
                dot_lt(rows_two, grad_up).astype(low),
                dot_lt(grad_rows, hidden).astype(low),
            ],
            axis=1,
        ).reshape(count, PLANE * shard, 3 * chunk)
        total, wait = scatter_line(grads, level, count, wait)
        ffn_grads.append(to_rows(total.astype(low), place))
    grad_normed_two = None
    for (grad_gate, grad_up), part in zip(grad_acts, chunk_weights):
        term = dot_rt(jnp.concatenate([grad_gate, grad_up], axis=1), part[:, : 2 * chunk])
        grad_normed_two = term if grad_normed_two is None else grad_normed_two + term
    grad_normed_two = scatter_plane(grad_normed_two)
    grad_unit_two, gain_two_part = norm_back(grad_normed_two, unit_two, scale_two, gain_second)
    grad_middle = cotangent.astype(f32) + grad_unit_two
    grad_branch = gather_plane(grad_middle.astype(low))
    down_all = jnp.concatenate([part[:, 2 * chunk :] for part in chunk_weights], axis=1)
    output = (middle + scatter_plane(dot_rt(jnp.concatenate(hiddens, axis=1), down_all))).astype(low)

    grad_mixed = dot(grad_branch, w_o).astype(low).reshape(PLANE, seq_len, heads, HEAD_DIM)
    grad_out = dot_lt(grad_branch, mixed).astype(low).reshape(count, PLANE * shard, width)
    grad_out, wait = scatter_line(grad_out, level, count, wait)
    grad_probs = jnp.einsum("nqhd,nkhd->nhqk", grad_mixed, values, preferred_element_type=f32)
    grad_dots = (grad_probs * probs * (1.0 - probs)).astype(low)
    grad_q = jnp.einsum("nhqk,nkhd->nqhd", grad_dots, keys, preferred_element_type=f32) * scale_dot
    grad_k = jnp.einsum("nhqk,nqhd->nkhd", grad_dots, queries, preferred_element_type=f32) * scale_dot
    grad_v = jnp.einsum("nhqk,nqhd->nkhd", probs_low, grad_mixed, preferred_element_type=f32)
    grad_qkv = jnp.concatenate(
        [
            unrotate(grad_q, cosine, sine).astype(low).reshape(PLANE * seq_len, width),
            unrotate(grad_k, cosine, sine).astype(low).reshape(PLANE * seq_len, width),
            grad_v.astype(low).reshape(PLANE * seq_len, width),
        ],
        axis=1,
    )
    grad_proj = dot_lt(rows_one, grad_qkv).astype(low).reshape(count, PLANE * shard, 3 * width)
    grad_proj, wait = scatter_line(grad_proj, level, count, wait)
    grad_normed_one = scatter_plane(dot_rt(grad_qkv, w_qkv))
    grad_unit_one, gain_one_part = norm_back(grad_normed_one, unit_one, scale_one, gain_first)
    grad_tokens = grad_middle + grad_unit_one

    out_rows = to_rows(grad_out.astype(low), place).astype(f32).reshape(shard, PLANE * width)
    proj_rows = to_rows(grad_proj.astype(low), place).astype(f32)
    proj = [
        proj_rows[:, :, k * width : (k + 1) * width].reshape(shard, PLANE * width) for k in range(3)
    ]
    ffn = [
        jnp.concatenate(
            [g[:, :, k * chunk : (k + 1) * chunk] for g in ffn_grads], axis=2
        )
        .astype(f32)
        .reshape(shard, PLANE * units)
        for k in range(3)
    ]
    return (
        output,
        grad_tokens,
        scatter_gain(gain_one_part, place, level, count),
        scatter_gain(gain_two_part, place, level, count),
        proj[0],
        proj[1],
        proj[2],
        out_rows,
        ffn[0],
        ffn[1],
        ffn[2],
    )


def solution(mesh):
    rows, grid = P(("dp", "tensor"), None), P("dp", "tensor")
    return jax.shard_map(
        local,
        mesh=mesh,
        in_specs=(rows, P("dp", None), P("dp"), P("dp")) + (grid,) * 7 + (rows,),
        out_specs=(rows, rows, P("dp"), P("dp")) + (grid,) * 7,
        check_vma=False,
    )
```

```python
import math

import jax
import jax.numpy as jnp
from jax import lax
from jax.sharding import Mesh
from jax.sharding import PartitionSpec as P

HEAD_DIM = 128
SEQ_LEN = 512
PLANE = 4
CHUNKS = 2

epsilon = 1e-05
theta = 10000.0
low = jnp.bfloat16
f32 = jnp.float32


def dot(left, right):
    return jnp.dot(left, right, preferred_element_type=f32)


def dot_rt(left, right):
    return lax.dot_general(left, right, (((1,), (1,)), ((), ())), preferred_element_type=f32)


def dot_lt(left, right):
    return lax.dot_general(left, right, (((0,), (0,)), ((), ())), preferred_element_type=f32)


def after(value, *earlier):
    return lax.optimization_barrier((value,) + earlier)[0]


def swap(value, axis):
    return lax.ppermute(value, axis, [(0, 1), (1, 0)])


def gather_plane(own):
    half = own.shape[0] // 2
    from_x = swap(own, "tensor")
    from_y = swap(own, "y")
    chip = jnp.concatenate(
        [own, from_x, from_y, swap(from_x[:half], "y"), swap(from_y[half:], "tensor")], axis=0
    )
    return jnp.concatenate([chip, swap(chip, "c")], axis=0)


def scatter_plane(partial):
    rows = partial.shape[0] // 8
    half = rows // 2
    width = partial.shape[1]
    mine, theirs = partial[: 4 * rows], partial[4 * rows :]
    both = mine.astype(f32) + swap(theirs.astype(low), "c").astype(f32)
    both = both.reshape(2, 2, rows, width)
    top, bottom = both[:, :, :half], both[:, :, half:]
    top_x = swap(top[:, 1].astype(low), "tensor")
    bottom_y = swap(bottom[1].astype(low), "y")
    top = top[:, 0] + top_x.astype(f32)
    bottom = bottom[0] + bottom_y.astype(f32)
    top_y = swap(top[1].astype(low), "y")
    bottom_x = swap(bottom[1].astype(low), "tensor")
    return jnp.concatenate([top[0] + top_y.astype(f32), bottom[0] + bottom_x.astype(f32)], axis=0)


def to_columns(parts):
    block = lax.all_to_all(parts, ("y", "c"), 0, 0, tiled=True)
    return block.reshape(-1, parts.shape[2])


def to_rows(block):
    parts = block.reshape(PLANE, block.shape[0] // PLANE, block.shape[1])
    return lax.all_to_all(parts, ("y", "c"), 0, 0, tiled=True)


def gather_line(block):
    return lax.all_gather(block, "z", axis=0, tiled=True)


def scatter_line(grads):
    return lax.psum_scatter(grads.astype(low), "z", scatter_dimension=0, tiled=True)


def quarters(weight, width):
    return jnp.swapaxes(weight.reshape(weight.shape[0], PLANE, width), 0, 1)


def shard_of(parts):
    return jnp.swapaxes(parts, 0, 1).reshape(parts.shape[1], -1).astype(f32)


def normalize(rows):
    scale = lax.rsqrt(jnp.mean(rows * rows, axis=-1, keepdims=True) + epsilon)
    return rows * scale, scale


def norm_back(grad_normed, unit_rows, scale, gain):
    inner = grad_normed * gain
    mean_term = jnp.mean(inner * unit_rows, axis=-1, keepdims=True)
    return scale * (inner - unit_rows * mean_term), jnp.sum(grad_normed * unit_rows, axis=0)


def rotate(values, cosine, sine):
    half = values.shape[-1] // 2
    first, second = values[..., :half], values[..., half:]
    return jnp.concatenate(
        [first * cosine - second * sine, second * cosine + first * sine], axis=-1
    )


def unrotate(values, cosine, sine):
    half = values.shape[-1] // 2
    first, second = values[..., :half], values[..., half:]
    return jnp.concatenate(
        [first * cosine + second * sine, second * cosine - first * sine], axis=-1
    )


def shifted(value, step):
    count = lax.axis_size("z")
    return lax.ppermute(value, "z", [(i, (i + step) % count) for i in range(count)])


def plane_flip(value, dy, dc):
    if dy and dc:
        return lax.ppermute(value, ("y", "c"), [(i, i ^ 3) for i in range(4)])
    return swap(value, "y" if dy else "c")


def gather_gains(gains, place, level):
    plane = jnp.zeros((PLANE,) + gains.shape, gains.dtype)
    for flip in range(PLANE):
        piece = plane_flip(gains, flip // 2, flip % 2) if flip else gains
        plane = lax.dynamic_update_index_in_dim(plane, piece, place ^ flip, 0)
    count = lax.axis_size("z")
    whole = jnp.zeros((count,) + plane.shape, gains.dtype)
    whole = lax.dynamic_update_index_in_dim(whole, plane, level, 0)
    for step in range(1, count):
        piece = shifted(plane, step)
        whole = lax.dynamic_update_index_in_dim(
            whole, piece, lax.rem(level - step + count, count), 0
        )
    return jnp.moveaxis(whole, 2, 0).reshape(gains.shape[0], -1)


def scatter_gain(part, place, level):
    count = lax.axis_size("z")
    part = part + swap(part, "tensor")
    blocks = part.reshape(count, PLANE, -1)
    mine = lax.dynamic_index_in_dim(blocks, place, 1, keepdims=False)
    for flip in range(1, PLANE):
        piece = lax.dynamic_index_in_dim(blocks, place ^ flip, 1, keepdims=False)
        mine = mine + plane_flip(piece, flip // 2, flip % 2)
    result = lax.dynamic_index_in_dim(mine, level, 0, keepdims=False)
    for step in range(1, count):
        piece = lax.dynamic_index_in_dim(mine, lax.rem(level + step, count), 0, keepdims=False)
        result = result + shifted(piece, step)
    return result


def local(
    tokens,
    segments,
    gain_attn,
    gain_ffn,
    w_query,
    w_key,
    w_value,
    w_out,
    w_gate,
    w_up,
    w_down,
    cotangent,
):
    seq_len = segments.shape[1]
    side = lax.axis_index("tensor")
    level, place = lax.axis_index("z"), lax.axis_index("y") * 2 + lax.axis_index("c")
    scale_dot = 1.0 / math.sqrt(HEAD_DIM)
    shift = -math.log(SEQ_LEN)
    width = w_query.shape[1] // PLANE
    heads = width // HEAD_DIM
    units = w_gate.shape[1] // PLANE
    chunk = units // CHUNKS

    attn_block = to_columns(
        jnp.concatenate([quarters(w, width) for w in (w_query, w_key, w_value, w_out)], axis=2)
    )
    attn_weights = gather_line(attn_block)
    w_qkv, w_o = attn_weights[:, : 3 * width], attn_weights[:, 3 * width :]
    chunk_weights = []
    wide = [quarters(w, units) for w in (w_gate, w_up, w_down)]
    earlier = attn_block
    for k in range(CHUNKS):
        parts = jnp.concatenate([w[:, :, k * chunk : (k + 1) * chunk] for w in wide], axis=2)
        earlier = to_columns(after(parts, earlier))
        chunk_weights.append(gather_line(earlier))

    gains = gather_gains(jnp.stack([gain_attn, gain_ffn]), place, level).astype(f32)
    gain_first, gain_second = gains[0], gains[1]
    inputs = tokens.astype(f32)
    unit_one, scale_one = normalize(inputs)
    rows_one = gather_plane((unit_one * gain_first).astype(low))
    grad_rows = gather_plane(after(cotangent, rows_one))
    seg = jnp.concatenate([segments] + [plane_flip(segments, dy, dc) for dc, dy in ((0, 1), (1, 0), (1, 1))], axis=0)
    places = lax.rem(jnp.arange(seq_len, dtype=jnp.int32) + side * (seq_len // 2), seq_len)
    seg = jnp.where(side == 0, seg, jnp.roll(seg, seq_len // 2, axis=1))
    same = seg[:, :, None] == seg[:, None, :]
    live = same & (places[None, None, :] <= places[None, :, None])
    positions = jnp.sum(live.astype(jnp.int32), axis=2) - 1
    freqs = theta ** (-(jnp.arange(HEAD_DIM // 2, dtype=f32) * 2.0 / HEAD_DIM))
    angles = positions.astype(f32)[..., None] * freqs
    cosine, sine = jnp.cos(angles)[:, :, None, :], jnp.sin(angles)[:, :, None, :]

    qkv = dot(rows_one, w_qkv).reshape(PLANE, seq_len, 3, heads, HEAD_DIM)
    queries = rotate(qkv[:, :, 0], cosine, sine).astype(low)
    keys = rotate(qkv[:, :, 1], cosine, sine).astype(low)
    values = qkv[:, :, 2].astype(low)

    def weights():
        dots = (
            jnp.einsum("nqhd,nkhd->nhqk", queries, keys, preferred_element_type=f32) * scale_dot
        )
        return jnp.where(live[:, None], jax.nn.sigmoid(dots + shift), 0.0)

    probs = weights()
    probs_low = probs.astype(low)
    mixed = jnp.einsum("nhqk,nkhd->nqhd", probs_low, values, preferred_element_type=f32)
    mixed = mixed.reshape(PLANE * seq_len, width).astype(low)
    middle = inputs + scatter_plane(dot_rt(mixed, w_o))
    unit_two, scale_two = normalize(middle)
    rows_two = gather_plane((unit_two * gain_second).astype(low))

    hiddens, grad_acts, grad_in, grad_downs = [], [], [], []
    for k in range(CHUNKS):
        part = chunk_weights[k]
        wg, wu, wd = part[:, :chunk], part[:, chunk : 2 * chunk], part[:, 2 * chunk :]
        gate = dot(rows_two, wg)
        upward = dot(rows_two, wu)
        grad_hidden = dot(grad_rows, wd)
        gate_sig = jax.nn.sigmoid(gate)
        silu = gate * gate_sig
        hidden = (silu * upward).astype(low)
        grad_gate = (grad_hidden * upward * gate_sig * (1.0 + gate * (1.0 - gate_sig))).astype(low)
        grad_up = (grad_hidden * silu).astype(low)
        hiddens.append(hidden)
        both = jnp.concatenate([grad_gate, grad_up], axis=1)
        grad_acts.append(both)
        grad_in.append(to_rows(scatter_line(dot_lt(rows_two, both))))
        grad_downs.append(to_rows(scatter_line(dot_lt(grad_rows, hidden))))
    grad_normed_two = None
    for both, part in zip(grad_acts, chunk_weights):
        term = dot_rt(both, part[:, : 2 * chunk])
        grad_normed_two = term if grad_normed_two is None else grad_normed_two + term
    grad_normed_two = scatter_plane(grad_normed_two)
    grad_unit_two, gain_two_part = norm_back(grad_normed_two, unit_two, scale_two, gain_second)
    grad_middle = cotangent.astype(f32) + grad_unit_two
    grad_branch = gather_plane(grad_middle.astype(low))
    down_all = jnp.concatenate([part[:, 2 * chunk :] for part in chunk_weights], axis=1)
    output = (middle + scatter_plane(dot_rt(jnp.concatenate(hiddens, axis=1), down_all))).astype(low)

    grad_mixed = dot(grad_branch, w_o).astype(low).reshape(PLANE, seq_len, heads, HEAD_DIM)
    grad_out = to_rows(scatter_line(dot_lt(grad_branch, mixed)))
    grad_probs = jnp.einsum("nqhd,nkhd->nhqk", grad_mixed, values, preferred_element_type=f32)
    grad_dots = (grad_probs * probs * (1.0 - probs)).astype(low)
    grad_q = jnp.einsum("nhqk,nkhd->nqhd", grad_dots, keys, preferred_element_type=f32) * scale_dot
    grad_k = jnp.einsum("nhqk,nqhd->nkhd", grad_dots, queries, preferred_element_type=f32) * scale_dot
    grad_v = jnp.einsum("nhqk,nqhd->nkhd", probs_low, grad_mixed, preferred_element_type=f32)
    grad_qkv = jnp.concatenate(
        [
            unrotate(grad_q, cosine, sine).astype(low).reshape(PLANE * seq_len, width),
            unrotate(grad_k, cosine, sine).astype(low).reshape(PLANE * seq_len, width),
            grad_v.astype(low).reshape(PLANE * seq_len, width),
        ],
        axis=1,
    )
    grad_proj = to_rows(scatter_line(dot_lt(rows_one, grad_qkv)))
    grad_normed_one = scatter_plane(dot_rt(grad_qkv, w_qkv))
    grad_unit_one, gain_one_part = norm_back(grad_normed_one, unit_one, scale_one, gain_first)
    grad_tokens = grad_middle + grad_unit_one

    proj = [shard_of(grad_proj[:, :, k * width : (k + 1) * width]) for k in range(3)]
    ffn = [
        shard_of(jnp.concatenate([g[:, :, k * chunk : (k + 1) * chunk] for g in grad_in], axis=2))
        for k in range(2)
    ]
    ffn.append(shard_of(jnp.concatenate(grad_downs, axis=2)))
    return (
        output,
        grad_tokens,
        scatter_gain(gain_one_part, place, level),
        scatter_gain(gain_two_part, place, level),
        proj[0],
        proj[1],
        proj[2],
        shard_of(grad_out),
        ffn[0],
        ffn[1],
        ffn[2],
    )


def solution(mesh):
    lines = mesh.shape["dp"] // PLANE
    finer = Mesh(
        mesh.devices.reshape(lines, 2, 2, mesh.shape["tensor"]), ("z", "y", "c", "tensor")
    )
    dp = ("z", "y", "c")
    rows, grid = P(dp + ("tensor",), None), P(dp, "tensor")
    return jax.shard_map(
        local,
        mesh=finer,
        in_specs=(rows, P(dp, None), P(dp), P(dp)) + (grid,) * 7 + (rows,),
        out_specs=(rows, rows, P(dp), P(dp)) + (grid,) * 7,
        check_vma=False,
    )
```

```python
import functools
import math

import jax
import jax.numpy as jnp
from jax import lax
from jax.experimental import pallas as pl
from jax.experimental.pallas import tpu as pltpu
from jax.sharding import Mesh
from jax.sharding import PartitionSpec as P

HEAD_DIM = 128
SEQ_LEN = 512
PLANE = 4
CHUNKS = 2

epsilon = 1e-05
theta = 10000.0
low = jnp.bfloat16
f32 = jnp.float32
params = pltpu.CompilerParams(vmem_limit_bytes=56 * 2**20)


def dot(left, right):
    return jnp.dot(left, right, preferred_element_type=f32)


def dot_rt(left, right):
    return lax.dot_general(left, right, (((1,), (1,)), ((), ())), preferred_element_type=f32)


def dot_lt(left, right):
    return lax.dot_general(left, right, (((0,), (0,)), ((), ())), preferred_element_type=f32)


def after(value, *earlier):
    return lax.optimization_barrier((value,) + earlier)[0]


def whole(array):
    return pl.BlockSpec(array.shape, lambda i: (0,) * array.ndim)


def cost(flops, *arrays):
    size = sum(math.prod(a.shape) * a.dtype.itemsize for a in arrays)
    return pl.CostEstimate(flops=flops, bytes_accessed=size, transcendentals=0)


def turn(vectors, cosine, sine):
    return vectors * cosine + pltpu.roll(vectors, HEAD_DIM // 2, 1) * sine


def weights_of(query, key, live):
    dots = dot_rt(query, key) * (1.0 / math.sqrt(HEAD_DIM)) - math.log(SEQ_LEN)
    return jax.nn.sigmoid(dots) * live


def attend_kernel(width, rows_ref, w_ref, cos_ref, sin_ref, live_ref, qkv_ref, mixed_ref, part_ref):
    qkv = dot(rows_ref[...], w_ref[:, : 3 * width])
    cosine, sine = cos_ref[...], sin_ref[...]
    live = live_ref[...].astype(f32)
    for first in range(0, width, HEAD_DIM):
        at_q, at_k, at_v = (slice(g + first, g + first + HEAD_DIM) for g in (0, width, 2 * width))
        query = turn(qkv[:, at_q], cosine, sine).astype(low)
        key = turn(qkv[:, at_k], cosine, sine).astype(low)
        value = qkv[:, at_v].astype(low)
        qkv_ref[:, at_q] = query
        qkv_ref[:, at_k] = key
        qkv_ref[:, at_v] = value
        probs = weights_of(query, key, live)
        mixed_ref[:, at_q] = dot(probs.astype(low), value).astype(low)
    part_ref[...] = dot_rt(mixed_ref[...], w_ref[:, 3 * width :]).astype(low)


def attend(rows, weights, cosine, sine, live):
    total, model = rows.shape
    width, seq = weights.shape[1] // 4, live.shape[1]
    tile = lambda columns: pl.BlockSpec((seq, columns), lambda n: (n, 0))
    outs = [jax.ShapeDtypeStruct((total, c), low) for c in (3 * width, width, model)]
    return pl.pallas_call(
        functools.partial(attend_kernel, width),
        grid=(total // seq,),
        in_specs=[tile(model), whole(weights), tile(HEAD_DIM), tile(HEAD_DIM), tile(seq)],
        out_specs=[tile(3 * width), tile(width), tile(model)],
        out_shape=outs,
        compiler_params=params,
        cost_estimate=cost(8 * total * model * width + 4 * total * seq * width, rows, weights, *outs),
    )(rows, weights, cosine, sine, live)


def attend_back_kernel(
    width, grad_ref, w_ref, qkv_ref, cos_ref, sin_ref, live_ref, grads_ref, part_ref
):
    grad_mixed = dot(grad_ref[...], w_ref[:, 3 * width :]).astype(low)
    cosine, sine = cos_ref[...], -sin_ref[...]
    live = live_ref[...].astype(f32)
    scale = 1.0 / math.sqrt(HEAD_DIM)
    for first in range(0, width, HEAD_DIM):
        at_q, at_k, at_v = (slice(g + first, g + first + HEAD_DIM) for g in (0, width, 2 * width))
        query, key, value = qkv_ref[:, at_q], qkv_ref[:, at_k], qkv_ref[:, at_v]
        grad = grad_mixed[:, at_q]
        probs = weights_of(query, key, live)
        grad_dots = (dot_rt(grad, value) * probs * (1.0 - probs)).astype(low)
        grads_ref[:, at_q] = turn(dot(grad_dots, key) * scale, cosine, sine).astype(low)
        grads_ref[:, at_k] = turn(dot_lt(grad_dots, query) * scale, cosine, sine).astype(low)
        grads_ref[:, at_v] = dot_lt(probs.astype(low), grad).astype(low)
    part_ref[...] = dot_rt(grads_ref[...], w_ref[:, : 3 * width]).astype(low)


def attend_back(grad_rows, weights, qkv, cosine, sine, live):
    total, model = grad_rows.shape
    width, seq = weights.shape[1] // 4, live.shape[1]
    tile = lambda columns: pl.BlockSpec((seq, columns), lambda n: (n, 0))
    outs = [jax.ShapeDtypeStruct((total, c), low) for c in (3 * width, model)]
    return pl.pallas_call(
        functools.partial(attend_back_kernel, width),
        grid=(total // seq,),
        in_specs=[
            tile(model),
            whole(weights),
            tile(3 * width),
            tile(HEAD_DIM),
            tile(HEAD_DIM),
            tile(seq),
        ],
        out_specs=[tile(3 * width), tile(model)],
        out_shape=outs,
        compiler_params=params,
        cost_estimate=cost(
            8 * total * model * width + 10 * total * seq * width, grad_rows, weights, qkv, *outs
        ),
    )(grad_rows, weights, qkv, cosine, sine, live)


def gated_kernel(units, rows_ref, grad_ref, w_ref, both_ref, hidden_ref):
    gate = dot(rows_ref[...], w_ref[:, :units])
    upward = dot(rows_ref[...], w_ref[:, units : 2 * units])
    grad_hidden = dot(grad_ref[...], w_ref[:, 2 * units :])
    gate_sig = jax.nn.sigmoid(gate)
    silu = gate * gate_sig
    both_ref[:, :units] = (
        grad_hidden * upward * gate_sig * (1.0 + gate * (1.0 - gate_sig))
    ).astype(low)
    both_ref[:, units:] = (grad_hidden * silu).astype(low)
    hidden_ref[...] = (silu * upward).astype(low)


def gated(rows, grad_rows, weights, tile=512):
    total, model = rows.shape
    units = weights.shape[1] // 3
    tiled = lambda columns: pl.BlockSpec((tile, columns), lambda i: (i, 0))
    outs = [jax.ShapeDtypeStruct((total, c), low) for c in (2 * units, units)]
    return pl.pallas_call(
        functools.partial(gated_kernel, units),
        grid=(total // tile,),
        in_specs=[tiled(model), tiled(model), whole(weights)],
        out_specs=[tiled(2 * units), tiled(units)],
        out_shape=outs,
        compiler_params=params,
        cost_estimate=cost(6 * total * model * units, rows, grad_rows, weights, *outs),
    )(rows, grad_rows, weights)


def project_kernel(first, count, *refs):
    total = None
    for act_ref, w_ref in zip(refs[:count], refs[count : 2 * count]):
        term = dot_rt(act_ref[...], w_ref[:, first : first + act_ref.shape[1]])
        total = term if total is None else total + term
    refs[-1][...] = total.astype(low)


def project(acts, weights, first, tile=256):
    total, wide = acts[0].shape
    model = weights[0].shape[0]
    out = jax.ShapeDtypeStruct((total, model), low)
    return pl.pallas_call(
        functools.partial(project_kernel, first, len(acts)),
        grid=(total // tile,),
        in_specs=[pl.BlockSpec((tile, wide), lambda i: (i, 0))] * len(acts)
        + [whole(w) for w in weights],
        out_specs=pl.BlockSpec((tile, model), lambda i: (i, 0)),
        out_shape=out,
        compiler_params=params,
        cost_estimate=cost(2 * total * model * wide * len(acts), *acts, *weights, out),
    )(*acts, *weights)


def outer_kernel(groups, *refs):
    out_ref = refs[-1]
    refs = list(refs[:-1])
    first = 0
    for count in groups:
        total = None
        for _ in range(count):
            left_ref, right_ref = refs.pop(0), refs.pop(0)
            term = dot_lt(left_ref[...], right_ref[...])
            total = term if total is None else total + term
        out_ref[:, first : first + total.shape[1]] = total.astype(low)
        first += total.shape[1]


def outer(*groups, tile=256):
    model = groups[0][0][0].shape[1]
    wide = sum(group[0][1].shape[1] for group in groups)
    out = jax.ShapeDtypeStruct((model, wide), low)
    operands, specs, flops = [], [], 0
    for group in groups:
        for left, right in group:
            operands += [left, right]
            specs += [pl.BlockSpec((left.shape[0], tile), lambda i: (0, i)), whole(right)]
            flops += 2 * left.shape[0] * model * right.shape[1]
    return pl.pallas_call(
        functools.partial(outer_kernel, [len(group) for group in groups]),
        grid=(model // tile,),
        in_specs=specs,
        out_specs=pl.BlockSpec((tile, wide), lambda i: (i, 0)),
        out_shape=out,
        compiler_params=params,
        cost_estimate=cost(flops, *operands, out),
    )(*operands)


def swap(value, axis):
    return lax.ppermute(value, axis, [(0, 1), (1, 0)])


def gather_plane(own):
    half = own.shape[0] // 2
    from_x = swap(own, "tensor")
    from_y = swap(own, "y")
    chip = jnp.concatenate(
        [own, from_x, from_y, swap(from_x[:half], "y"), swap(from_y[half:], "tensor")], axis=0
    )
    return chip, swap(chip, "c")


def scatter_plane(mine, theirs):
    rows = mine.shape[0] // 4
    half = rows // 2
    other = swap(theirs, "c")

    def piece(dy, dx, bottom):
        first = (2 * dy + dx) * rows + bottom * half
        return mine[first : first + half].astype(f32) + other[first : first + half].astype(f32)

    top_x = swap(jnp.concatenate([piece(0, 1, 0), piece(1, 1, 0)], axis=0).astype(low), "tensor")
    bottom_y = swap(jnp.concatenate([piece(1, 0, 1), piece(1, 1, 1)], axis=0).astype(low), "y")
    top_y = swap((piece(1, 0, 0) + top_x[half:].astype(f32)).astype(low), "y")
    bottom_x = swap((piece(0, 1, 1) + bottom_y[half:].astype(f32)).astype(low), "tensor")
    top = piece(0, 0, 0) + top_x[:half].astype(f32) + top_y.astype(f32)
    bottom = piece(0, 0, 1) + bottom_y[:half].astype(f32) + bottom_x.astype(f32)
    return jnp.concatenate([top, bottom], axis=0)


def to_columns(parts):
    block = lax.all_to_all(parts, ("y", "c"), 0, 0, tiled=True)
    return block.reshape(-1, parts.shape[2])


def to_rows(block):
    parts = block.reshape(PLANE, block.shape[0] // PLANE, block.shape[1])
    return lax.all_to_all(parts, ("y", "c"), 0, 0, tiled=True)


def gather_line(block):
    return lax.all_gather(block, "z", axis=0, tiled=True)


def scatter_line(grads):
    return lax.psum_scatter(grads, "z", scatter_dimension=0, tiled=True)


def quarters(weight, width):
    return jnp.swapaxes(weight.reshape(weight.shape[0], PLANE, width), 0, 1)


def shard_of(parts):
    return jnp.swapaxes(parts, 0, 1).reshape(parts.shape[1], -1).astype(f32)


def shifted(value, step):
    count = lax.axis_size("z")
    return lax.ppermute(value, "z", [(i, (i + step) % count) for i in range(count)])


def plane_flip(value, dy, dc):
    if dy and dc:
        return lax.ppermute(value, ("y", "c"), [(i, i ^ 3) for i in range(4)])
    return swap(value, "y" if dy else "c")


def gather_gains(gains, place, level):
    plane = jnp.zeros((PLANE,) + gains.shape, gains.dtype)
    for flip in range(PLANE):
        piece = plane_flip(gains, flip // 2, flip % 2) if flip else gains
        plane = lax.dynamic_update_index_in_dim(plane, piece, place ^ flip, 0)
    count = lax.axis_size("z")
    every = jnp.zeros((count,) + plane.shape, gains.dtype)
    every = lax.dynamic_update_index_in_dim(every, plane, level, 0)
    for step in range(1, count):
        piece = shifted(plane, step)
        every = lax.dynamic_update_index_in_dim(
            every, piece, lax.rem(level - step + count, count), 0
        )
    return jnp.moveaxis(every, 2, 0).reshape(gains.shape[0], -1)


def scatter_gains(part, place, level):
    count = lax.axis_size("z")
    part = part + swap(part, "tensor")
    blocks = part.reshape(part.shape[0], count, PLANE, -1)
    mine = lax.dynamic_index_in_dim(blocks, place, 2, keepdims=False)
    for flip in range(1, PLANE):
        piece = lax.dynamic_index_in_dim(blocks, place ^ flip, 2, keepdims=False)
        mine = mine + plane_flip(piece, flip // 2, flip % 2)
    result = lax.dynamic_index_in_dim(mine, level, 1, keepdims=False)
    for step in range(1, count):
        piece = lax.dynamic_index_in_dim(mine, lax.rem(level + step, count), 1, keepdims=False)
        result = result + shifted(piece, step)
    return result


def normalize(rows):
    scale = lax.rsqrt(jnp.mean(rows * rows, axis=-1, keepdims=True) + epsilon)
    return rows * scale, scale


def norm_back(grad_normed, unit_rows, scale, gain):
    inner = grad_normed * gain
    mean_term = jnp.mean(inner * unit_rows, axis=-1, keepdims=True)
    return scale * (inner - unit_rows * mean_term), jnp.sum(grad_normed * unit_rows, axis=0)


def local(
    tokens,
    segments,
    gain_attn,
    gain_ffn,
    w_query,
    w_key,
    w_value,
    w_out,
    w_gate,
    w_up,
    w_down,
    cotangent,
):
    seq_len = segments.shape[1]
    side = lax.axis_index("tensor")
    level, place = lax.axis_index("z"), lax.axis_index("y") * 2 + lax.axis_index("c")
    width = w_query.shape[1] // PLANE
    units = w_gate.shape[1] // PLANE
    chunk = units // CHUNKS

    attn_block = to_columns(
        jnp.concatenate([quarters(w, width) for w in (w_query, w_key, w_value, w_out)], axis=2)
    )
    attn_weights = gather_line(attn_block)
    wide = [quarters(w, units) for w in (w_gate, w_up, w_down)]
    ffn_parts = jnp.concatenate(
        [w[:, :, k * chunk : (k + 1) * chunk] for k in range(CHUNKS) for w in wide], axis=2
    )
    ffn_block = to_columns(after(ffn_parts, attn_block))
    ffn_weights = [
        gather_line(ffn_block[:, 3 * k * chunk : 3 * (k + 1) * chunk]) for k in range(CHUNKS)
    ]

    gains = gather_gains(jnp.stack([gain_attn, gain_ffn]), place, level).astype(f32)
    gain_first, gain_second = gains[0], gains[1]
    inputs = tokens.astype(f32)
    unit_one, scale_one = normalize(inputs)
    rows_one = gather_plane((unit_one * gain_first).astype(low))
    grad_rows = gather_plane(after(cotangent, rows_one[0]))
    seg = jnp.concatenate(
        [segments] + [plane_flip(segments, dy, dc) for dc, dy in ((0, 1), (1, 0), (1, 1))], axis=0
    )
    places = lax.rem(jnp.arange(seq_len, dtype=jnp.int32) + side * (seq_len // 2), seq_len)
    seg = jnp.where(side == 0, seg, jnp.roll(seg, seq_len // 2, axis=1))
    same = seg[:, :, None] == seg[:, None, :]
    live = same & (places[None, None, :] <= places[None, :, None])
    positions = jnp.sum(live.astype(jnp.int32), axis=2) - 1
    freqs = theta ** (-(jnp.arange(HEAD_DIM // 2, dtype=f32) * 2.0 / HEAD_DIM))
    angles = (positions.astype(f32)[..., None] * freqs).reshape(2, -1, HEAD_DIM // 2)
    cosine, sine = jnp.cos(angles), jnp.sin(angles)
    cosine = jnp.concatenate([cosine, cosine], axis=2)
    sine = jnp.concatenate([-sine, sine], axis=2)
    live = live.astype(low).reshape(2, -1, seq_len)
    sides = range(2)

    qkv, mixed, parts = zip(
        *(attend(rows_one[i], attn_weights, cosine[i], sine[i], live[i]) for i in sides)
    )
    middle = inputs + scatter_plane(*parts)
    unit_two, scale_two = normalize(middle)
    rows_two = gather_plane((unit_two * gain_second).astype(low))

    both = [[None] * CHUNKS for _ in sides]
    hidden = [[None] * CHUNKS for _ in sides]
    ffn_sums = []
    grad_parts = None
    for k in range(CHUNKS):
        for i in sides:
            both[i][k], hidden[i][k] = gated(rows_two[i], grad_rows[i], ffn_weights[k])
        if k == CHUNKS - 1:
            grad_parts = [project(both[i], ffn_weights, 0) for i in sides]
        sums = outer(
            [(rows_two[i], both[i][k]) for i in sides],
            [(grad_rows[i], hidden[i][k]) for i in sides],
        )
        ffn_sums.append(to_rows(scatter_line(sums)))
    grad_normed_two = scatter_plane(*grad_parts)
    grad_unit_two, gain_two_part = norm_back(grad_normed_two, unit_two, scale_two, gain_second)
    grad_middle = cotangent.astype(f32) + grad_unit_two
    grad_branch = gather_plane(after(grad_middle.astype(low), sums))

    grads, parts = zip(
        *(
            attend_back(grad_branch[i], attn_weights, qkv[i], cosine[i], sine[i], live[i])
            for i in sides
        )
    )
    attn_sums = to_rows(
        scatter_line(
            outer(
                [(rows_one[i], grads[i]) for i in sides],
                [(grad_branch[i], mixed[i]) for i in sides],
            )
        )
    )
    grad_normed_one = scatter_plane(*parts)
    grad_unit_one, gain_one_part = norm_back(grad_normed_one, unit_one, scale_one, gain_first)
    grad_tokens = grad_middle + grad_unit_one
    out_parts = [project(after(hidden[i], grad_branch[1]), ffn_weights, 2 * chunk) for i in sides]
    output = (middle + scatter_plane(*out_parts)).astype(low)
    gain_sums = scatter_gains(jnp.stack([gain_one_part, gain_two_part]), place, level)

    attn_grads = [shard_of(attn_sums[:, :, k * width : (k + 1) * width]) for k in range(4)]
    ffn_grads = [
        shard_of(jnp.concatenate([s[:, :, k * chunk : (k + 1) * chunk] for s in ffn_sums], axis=2))
        for k in range(3)
    ]
    return (output, grad_tokens, gain_sums[0], gain_sums[1], *attn_grads, *ffn_grads)


def solution(mesh):
    lines = mesh.shape["dp"] // PLANE
    finer = Mesh(
        mesh.devices.reshape(lines, 2, 2, mesh.shape["tensor"]), ("z", "y", "c", "tensor")
    )
    dp = ("z", "y", "c")
    rows, grid = P(dp + ("tensor",), None), P(dp, "tensor")
    return jax.shard_map(
        local,
        mesh=finer,
        in_specs=(rows, P(dp, None), P(dp), P(dp)) + (grid,) * 7 + (rows,),
        out_specs=(rows, rows, P(dp), P(dp)) + (grid,) * 7,
        check_vma=False,
    )
```

```python
import functools
import math

import jax
import jax.numpy as jnp
from jax import lax
from jax.experimental import pallas as pl
from jax.experimental.pallas import tpu as pltpu
from jax.sharding import Mesh
from jax.sharding import PartitionSpec as P

HEAD_DIM = 128
SEQ_LEN = 512
PLANE = 4
CHUNKS = 2

epsilon = 1e-05
theta = 10000.0
low = jnp.bfloat16
f32 = jnp.float32
params = pltpu.CompilerParams(vmem_limit_bytes=56 * 2**20)


def dot(left, right):
    return jnp.dot(left, right, preferred_element_type=f32)


def dot_rt(left, right):
    return lax.dot_general(left, right, (((1,), (1,)), ((), ())), preferred_element_type=f32)


def dot_lt(left, right):
    return lax.dot_general(left, right, (((0,), (0,)), ((), ())), preferred_element_type=f32)


def after(value, *earlier):
    return lax.optimization_barrier((value,) + earlier)[0]


def together(*values):
    return lax.optimization_barrier(values)


def whole(array):
    return pl.BlockSpec(array.shape, lambda i: (0,) * array.ndim)


def cost(flops, *arrays):
    size = sum(math.prod(a.shape) * a.dtype.itemsize for a in arrays)
    return pl.CostEstimate(flops=flops, bytes_accessed=size, transcendentals=0)


def turn(vectors, cosine, sine):
    return vectors * cosine + pltpu.roll(vectors, HEAD_DIM // 2, 1) * sine


def weights_of(query, key, live):
    dots = dot_rt(query, key) * (1.0 / math.sqrt(HEAD_DIM)) - math.log(SEQ_LEN)
    return jax.nn.sigmoid(dots) * live


def attend_kernel(width, rows_ref, w_ref, cos_ref, sin_ref, live_ref, qkv_ref, mixed_ref, part_ref):
    qkv = dot(rows_ref[...], w_ref[:, : 3 * width])
    cosine, sine = cos_ref[...], sin_ref[...]
    live = live_ref[...].astype(f32)
    for first in range(0, width, HEAD_DIM):
        at_q, at_k, at_v = (slice(g + first, g + first + HEAD_DIM) for g in (0, width, 2 * width))
        query = turn(qkv[:, at_q], cosine, sine).astype(low)
        key = turn(qkv[:, at_k], cosine, sine).astype(low)
        value = qkv[:, at_v].astype(low)
        qkv_ref[:, at_q] = query
        qkv_ref[:, at_k] = key
        qkv_ref[:, at_v] = value
        probs = weights_of(query, key, live)
        mixed_ref[:, at_q] = dot(probs.astype(low), value).astype(low)
    part_ref[...] = dot_rt(mixed_ref[...], w_ref[:, 3 * width :]).astype(low)


def attend(rows, weights, cosine, sine, live):
    total, model = rows.shape
    width, seq = weights.shape[1] // 4, live.shape[1]
    tile = lambda columns: pl.BlockSpec((seq, columns), lambda n: (n, 0))
    outs = [jax.ShapeDtypeStruct((total, c), low) for c in (3 * width, width, model)]
    return pl.pallas_call(
        functools.partial(attend_kernel, width),
        grid=(total // seq,),
        in_specs=[tile(model), whole(weights), tile(HEAD_DIM), tile(HEAD_DIM), tile(seq)],
        out_specs=[tile(3 * width), tile(width), tile(model)],
        out_shape=outs,
        compiler_params=params,
        cost_estimate=cost(8 * total * model * width + 4 * total * seq * width, rows, weights, *outs),
    )(rows, weights, cosine, sine, live)


def attend_back_kernel(
    width, grad_ref, w_ref, qkv_ref, cos_ref, sin_ref, live_ref, grads_ref, part_ref
):
    grad_mixed = dot(grad_ref[...], w_ref[:, 3 * width :]).astype(low)
    cosine, sine = cos_ref[...], -sin_ref[...]
    live = live_ref[...].astype(f32)
    scale = 1.0 / math.sqrt(HEAD_DIM)
    for first in range(0, width, HEAD_DIM):
        at_q, at_k, at_v = (slice(g + first, g + first + HEAD_DIM) for g in (0, width, 2 * width))
        query, key, value = qkv_ref[:, at_q], qkv_ref[:, at_k], qkv_ref[:, at_v]
        grad = grad_mixed[:, at_q]
        probs = weights_of(query, key, live)
        grad_dots = (dot_rt(grad, value) * probs * (1.0 - probs)).astype(low)
        grads_ref[:, at_q] = turn(dot(grad_dots, key) * scale, cosine, sine).astype(low)
        grads_ref[:, at_k] = turn(dot_lt(grad_dots, query) * scale, cosine, sine).astype(low)
        grads_ref[:, at_v] = dot_lt(probs.astype(low), grad).astype(low)
    part_ref[...] = dot_rt(grads_ref[...], w_ref[:, : 3 * width]).astype(low)


def attend_back(grad_rows, weights, qkv, cosine, sine, live):
    total, model = grad_rows.shape
    width, seq = weights.shape[1] // 4, live.shape[1]
    tile = lambda columns: pl.BlockSpec((seq, columns), lambda n: (n, 0))
    outs = [jax.ShapeDtypeStruct((total, c), low) for c in (3 * width, model)]
    return pl.pallas_call(
        functools.partial(attend_back_kernel, width),
        grid=(total // seq,),
        in_specs=[
            tile(model),
            whole(weights),
            tile(3 * width),
            tile(HEAD_DIM),
            tile(HEAD_DIM),
            tile(seq),
        ],
        out_specs=[tile(3 * width), tile(model)],
        out_shape=outs,
        compiler_params=params,
        cost_estimate=cost(
            8 * total * model * width + 10 * total * seq * width, grad_rows, weights, qkv, *outs
        ),
    )(grad_rows, weights, qkv, cosine, sine, live)


def gated_kernel(units, rows_ref, grad_ref, w_ref, both_ref, hidden_ref):
    gate = dot(rows_ref[...], w_ref[:, :units])
    upward = dot(rows_ref[...], w_ref[:, units : 2 * units])
    grad_hidden = dot(grad_ref[...], w_ref[:, 2 * units :])
    gate_sig = jax.nn.sigmoid(gate)
    silu = gate * gate_sig
    both_ref[:, :units] = (
        grad_hidden * upward * gate_sig * (1.0 + gate * (1.0 - gate_sig))
    ).astype(low)
    both_ref[:, units:] = (grad_hidden * silu).astype(low)
    hidden_ref[...] = (silu * upward).astype(low)


def gated(rows, grad_rows, weights, tile=512):
    total, model = rows.shape
    units = weights.shape[1] // 3
    tiled = lambda columns: pl.BlockSpec((tile, columns), lambda i: (i, 0))
    outs = [jax.ShapeDtypeStruct((total, c), low) for c in (2 * units, units)]
    return pl.pallas_call(
        functools.partial(gated_kernel, units),
        grid=(total // tile,),
        in_specs=[tiled(model), tiled(model), whole(weights)],
        out_specs=[tiled(2 * units), tiled(units)],
        out_shape=outs,
        compiler_params=params,
        cost_estimate=cost(6 * total * model * units, rows, grad_rows, weights, *outs),
    )(rows, grad_rows, weights)


def project_kernel(first, count, *refs):
    total = None
    for act_ref, w_ref in zip(refs[:count], refs[count : 2 * count]):
        term = dot_rt(act_ref[...], w_ref[:, first : first + act_ref.shape[1]])
        total = term if total is None else total + term
    refs[-1][...] = total.astype(low)


def project(acts, weights, first, tile=256):
    total, wide = acts[0].shape
    model = weights[0].shape[0]
    out = jax.ShapeDtypeStruct((total, model), low)
    return pl.pallas_call(
        functools.partial(project_kernel, first, len(acts)),
        grid=(total // tile,),
        in_specs=[pl.BlockSpec((tile, wide), lambda i: (i, 0))] * len(acts)
        + [whole(w) for w in weights],
        out_specs=pl.BlockSpec((tile, model), lambda i: (i, 0)),
        out_shape=out,
        compiler_params=params,
        cost_estimate=cost(2 * total * model * wide * len(acts), *acts, *weights, out),
    )(*acts, *weights)


def outer_kernel(groups, *refs):
    out_ref = refs[-1]
    refs = list(refs[:-1])
    first = 0
    for count in groups:
        total = None
        for _ in range(count):
            left_ref, right_ref = refs.pop(0), refs.pop(0)
            term = dot_lt(left_ref[...], right_ref[...])
            total = term if total is None else total + term
        out_ref[:, first : first + total.shape[1]] = total.astype(low)
        first += total.shape[1]


def outer(*groups, tile=256):
    model = groups[0][0][0].shape[1]
    wide = sum(group[0][1].shape[1] for group in groups)
    out = jax.ShapeDtypeStruct((model, wide), low)
    operands, specs, flops = [], [], 0
    for group in groups:
        for left, right in group:
            operands += [left, right]
            specs += [pl.BlockSpec((left.shape[0], tile), lambda i: (0, i)), whole(right)]
            flops += 2 * left.shape[0] * model * right.shape[1]
    return pl.pallas_call(
        functools.partial(outer_kernel, [len(group) for group in groups]),
        grid=(model // tile,),
        in_specs=specs,
        out_specs=pl.BlockSpec((tile, wide), lambda i: (i, 0)),
        out_shape=out,
        compiler_params=params,
        cost_estimate=cost(flops, *operands, out),
    )(*operands)


def swap(value, axis):
    return lax.ppermute(value, axis, [(0, 1), (1, 0)])


def gather_first(own):
    half = own.shape[0] // 2
    from_x, from_y = together(swap(own, "tensor"), swap(own, "y"))
    return own, from_x, from_y, (from_x[:half], from_y[half:])


def gather_last(state):
    own, from_x, from_y, (top, bottom) = state
    top, bottom = together(swap(top, "y"), swap(bottom, "tensor"))
    chip = jnp.concatenate([own, from_x, from_y, top, bottom], axis=0)
    return chip, swap(chip, "c")


def scatter_first(mine, theirs):
    rows = mine.shape[0] // 4
    half = rows // 2
    other = swap(theirs, "c")

    def piece(dy, dx, bottom):
        first = (2 * dy + dx) * rows + bottom * half
        return mine[first : first + half].astype(f32) + other[first : first + half].astype(f32)

    top_x = jnp.concatenate([piece(0, 1, 0), piece(1, 1, 0)], axis=0).astype(low)
    bottom_y = jnp.concatenate([piece(1, 0, 1), piece(1, 1, 1)], axis=0).astype(low)
    return piece, half, together(top_x, bottom_y)


def scatter_second(state):
    piece, half, (top_x, bottom_y) = state
    top_x, bottom_y = together(swap(top_x, "tensor"), swap(bottom_y, "y"))
    top_y = (piece(1, 0, 0) + top_x[half:].astype(f32)).astype(low)
    bottom_x = (piece(0, 1, 1) + bottom_y[half:].astype(f32)).astype(low)
    return piece, half, (top_x[:half], bottom_y[:half], top_y, bottom_x)


def scatter_last(state):
    piece, half, (top_x, bottom_y, top_y, bottom_x) = state
    top_y, bottom_x = together(swap(top_y, "y"), swap(bottom_x, "tensor"))
    top = piece(0, 0, 0) + top_x.astype(f32) + top_y.astype(f32)
    bottom = piece(0, 0, 1) + bottom_y.astype(f32) + bottom_x.astype(f32)
    return jnp.concatenate([top, bottom], axis=0)


def beside(state, *others):
    sends, *others = together(state[-1], *others)
    return (*state[:-1], sends), *others


def to_columns(parts):
    block = lax.all_to_all(parts, ("y", "c"), 0, 0, tiled=True)
    return block.reshape(-1, parts.shape[2])


def to_rows(block):
    parts = block.reshape(PLANE, block.shape[0] // PLANE, block.shape[1])
    return lax.all_to_all(parts, ("y", "c"), 0, 0, tiled=True)


def gather_line(block):
    return lax.all_gather(block, "z", axis=0, tiled=True)


def scatter_line(grads):
    return lax.psum_scatter(grads, "z", scatter_dimension=0, tiled=True)


def quarters(weight, width):
    return jnp.swapaxes(weight.reshape(weight.shape[0], PLANE, width), 0, 1)


def shard_of(parts):
    return jnp.swapaxes(parts, 0, 1).reshape(parts.shape[1], -1).astype(f32)


def shifted(value, step):
    count = lax.axis_size("z")
    return lax.ppermute(value, "z", [(i, (i + step) % count) for i in range(count)])


def plane_flip(value, dy, dc):
    if dy and dc:
        return lax.ppermute(value, ("y", "c"), [(i, i ^ 3) for i in range(4)])
    return swap(value, "y" if dy else "c")


def gather_gains(gains, place, level):
    plane = jnp.zeros((PLANE,) + gains.shape, gains.dtype)
    for flip in range(PLANE):
        piece = plane_flip(gains, flip // 2, flip % 2) if flip else gains
        plane = lax.dynamic_update_index_in_dim(plane, piece, place ^ flip, 0)
    count = lax.axis_size("z")
    every = jnp.zeros((count,) + plane.shape, gains.dtype)
    every = lax.dynamic_update_index_in_dim(every, plane, level, 0)
    for step in range(1, count):
        piece = shifted(plane, step)
        every = lax.dynamic_update_index_in_dim(
            every, piece, lax.rem(level - step + count, count), 0
        )
    return jnp.moveaxis(every, 2, 0).reshape(gains.shape[0], -1)


def scatter_gains(part, place, level):
    count = lax.axis_size("z")
    part = part + swap(part, "tensor")
    blocks = part.reshape(part.shape[0], count, PLANE, -1)
    mine = lax.dynamic_index_in_dim(blocks, place, 2, keepdims=False)
    for flip in range(1, PLANE):
        piece = lax.dynamic_index_in_dim(blocks, place ^ flip, 2, keepdims=False)
        mine = mine + plane_flip(piece, flip // 2, flip % 2)
    result = lax.dynamic_index_in_dim(mine, level, 1, keepdims=False)
    for step in range(1, count):
        piece = lax.dynamic_index_in_dim(mine, lax.rem(level + step, count), 1, keepdims=False)
        result = result + shifted(piece, step)
    return result


def normalize(rows):
    scale = lax.rsqrt(jnp.mean(rows * rows, axis=-1, keepdims=True) + epsilon)
    return rows * scale, scale


def norm_back(grad_normed, unit_rows, scale, gain):
    inner = grad_normed * gain
    mean_term = jnp.mean(inner * unit_rows, axis=-1, keepdims=True)
    return scale * (inner - unit_rows * mean_term), jnp.sum(grad_normed * unit_rows, axis=0)


def local(
    tokens,
    segments,
    gain_attn,
    gain_ffn,
    w_query,
    w_key,
    w_value,
    w_out,
    w_gate,
    w_up,
    w_down,
    cotangent,
):
    seq_len = segments.shape[1]
    side = lax.axis_index("tensor")
    level, place = lax.axis_index("z"), lax.axis_index("y") * 2 + lax.axis_index("c")
    width = w_query.shape[1] // PLANE
    units = w_gate.shape[1] // PLANE
    chunk = units // CHUNKS

    attn_block = to_columns(
        jnp.concatenate([quarters(w, width) for w in (w_query, w_key, w_value, w_out)], axis=2)
    )
    attn_weights = gather_line(attn_block)
    wide = [quarters(w, units) for w in (w_gate, w_up, w_down)]
    ffn_parts = jnp.concatenate(
        [w[:, :, k * chunk : (k + 1) * chunk] for k in range(CHUNKS) for w in wide], axis=2
    )
    ffn_block = to_columns(ffn_parts)

    gains = gather_gains(jnp.stack([gain_attn, gain_ffn]), place, level)
    seg = jnp.concatenate(
        [segments] + [plane_flip(segments, dy, dc) for dc, dy in ((0, 1), (1, 0), (1, 1))], axis=0
    )
    gains, seg = together(gains, seg)
    gain_first, gain_second = gains[0].astype(f32), gains[1].astype(f32)
    inputs = tokens.astype(f32)
    unit_one, scale_one = normalize(inputs)
    places = lax.rem(jnp.arange(seq_len, dtype=jnp.int32) + side * (seq_len // 2), seq_len)
    seg = jnp.where(side == 0, seg, jnp.roll(seg, seq_len // 2, axis=1))
    same = seg[:, :, None] == seg[:, None, :]
    live = same & (places[None, None, :] <= places[None, :, None])
    positions = jnp.sum(live.astype(jnp.int32), axis=2) - 1
    freqs = theta ** (-(jnp.arange(HEAD_DIM // 2, dtype=f32) * 2.0 / HEAD_DIM))
    angles = (positions.astype(f32)[..., None] * freqs).reshape(2, -1, HEAD_DIM // 2)
    cosine, sine = jnp.cos(angles), jnp.sin(angles)
    cosine = jnp.concatenate([cosine, cosine], axis=2)
    sine = jnp.concatenate([-sine, sine], axis=2)
    live = live.astype(low).reshape(2, -1, seq_len)
    sides = range(2)
    state, live, cosine, sine, ffn_block = beside(
        gather_first((unit_one * gain_first).astype(low)), live, cosine, sine, ffn_block
    )
    rows_one = gather_last(state)
    ffn_weights = [
        gather_line(ffn_block[:, 3 * k * chunk : 3 * (k + 1) * chunk]) for k in range(CHUNKS)
    ]
    grad_own, attn_weights = together(cotangent, attn_weights)

    qkv, mixed, parts = zip(
        *(attend(rows_one[i], attn_weights, cosine[i], sine[i], live[i]) for i in sides)
    )
    grad_state, parts = beside(gather_first(grad_own), parts)
    middle = inputs + scatter_last(scatter_second(scatter_first(*parts)))
    unit_two, scale_two = normalize(middle)
    rows_two = gather_last(gather_first((unit_two * gain_second).astype(low)))
    grad_state, rows_own = beside(grad_state, rows_two[0])
    rows_two = (rows_own, rows_two[1])
    grad_rows = gather_last(grad_state)

    both = [[None] * CHUNKS for _ in sides]
    hidden = [[None] * CHUNKS for _ in sides]
    ffn_sums = []
    grad_parts = None
    for k in range(CHUNKS):
        for i in sides:
            both[i][k], hidden[i][k] = gated(rows_two[i], grad_rows[i], ffn_weights[k])
        if k == CHUNKS - 1:
            grad_parts = [project(both[i], ffn_weights, 0) for i in sides]
        sums = outer(
            [(rows_two[i], both[i][k]) for i in sides],
            [(grad_rows[i], hidden[i][k]) for i in sides],
        )
        if k == CHUNKS - 1:
            grad_state, sums = beside(scatter_second(scatter_first(*grad_parts)), sums)
        ffn_sums.append(scatter_line(sums))
    grad_normed_two = scatter_last(grad_state)
    grad_unit_two, gain_two_part = norm_back(grad_normed_two, unit_two, scale_two, gain_second)
    grad_middle = cotangent.astype(f32) + grad_unit_two
    grad_branch = gather_first(grad_middle.astype(low))
    out_parts = [project(hidden[i], ffn_weights, 2 * chunk) for i in sides]
    grad_branch, out_parts = beside(grad_branch, out_parts)
    grad_branch = gather_last(grad_branch)
    out_state, grad_own = beside(scatter_first(*out_parts), grad_branch[0])
    grad_branch = (grad_own, grad_branch[1])

    grads, parts = zip(
        *(
            attend_back(grad_branch[i], attn_weights, qkv[i], cosine[i], sine[i], live[i])
            for i in sides
        )
    )
    ffn_rows = [to_rows(ffn_sums[0])]
    out_state, grads, ffn_rows = beside(scatter_second(out_state), grads, ffn_rows)
    sums = outer(
        [(rows_one[i], grads[i]) for i in sides],
        [(grad_branch[i], mixed[i]) for i in sides],
    )
    sums, out_sums = together(sums, scatter_last(out_state))
    attn_sums = to_rows(scatter_line(sums))
    output = (middle + out_sums).astype(low)
    grad_normed_one = scatter_last(scatter_second(scatter_first(*parts)))
    ffn_rows += [to_rows(s) for s in ffn_sums[1:]]
    grad_unit_one, gain_one_part = norm_back(grad_normed_one, unit_one, scale_one, gain_first)
    grad_tokens = grad_middle + grad_unit_one
    gain_sums = scatter_gains(jnp.stack([gain_one_part, gain_two_part]), place, level)

    attn_grads = [shard_of(attn_sums[:, :, k * width : (k + 1) * width]) for k in range(4)]
    ffn_grads = [
        shard_of(jnp.concatenate([s[:, :, k * chunk : (k + 1) * chunk] for s in ffn_rows], axis=2))
        for k in range(3)
    ]
    return (output, grad_tokens, gain_sums[0], gain_sums[1], *attn_grads, *ffn_grads)


def solution(mesh):
    lines = mesh.shape["dp"] // PLANE
    finer = Mesh(
        mesh.devices.reshape(lines, 2, 2, mesh.shape["tensor"]), ("z", "y", "c", "tensor")
    )
    dp = ("z", "y", "c")
    rows, grid = P(dp + ("tensor",), None), P(dp, "tensor")
    return jax.shard_map(
        local,
        mesh=finer,
        in_specs=(rows, P(dp, None), P(dp), P(dp)) + (grid,) * 7 + (rows,),
        out_specs=(rows, rows, P(dp), P(dp)) + (grid,) * 7,
        check_vma=False,
    )
```

```python
import functools
import math

import jax
import jax.numpy as jnp
from jax import lax
from jax.experimental import pallas as pl
from jax.experimental.pallas import tpu as pltpu
from jax.sharding import Mesh
from jax.sharding import PartitionSpec as P

HEAD_DIM = 128
SEQ_LEN = 512
PLANE = 4
CHUNKS = 2

epsilon = 1e-05
theta = 10000.0
low = jnp.bfloat16
f32 = jnp.float32
params = pltpu.CompilerParams(vmem_limit_bytes=56 * 2**20)


def dot(left, right):
    return jnp.dot(left, right, preferred_element_type=f32)


def dot_rt(left, right):
    return lax.dot_general(left, right, (((1,), (1,)), ((), ())), preferred_element_type=f32)


def dot_lt(left, right):
    return lax.dot_general(left, right, (((0,), (0,)), ((), ())), preferred_element_type=f32)


def after(value, *earlier):
    return lax.optimization_barrier((value,) + earlier)[0]


def together(*values):
    return lax.optimization_barrier(values)


def whole(array):
    return pl.BlockSpec(array.shape, lambda i: (0,) * array.ndim)


def cost(flops, *arrays):
    size = sum(math.prod(a.shape) * a.dtype.itemsize for a in arrays)
    return pl.CostEstimate(flops=flops, bytes_accessed=size, transcendentals=0)


def turn(vectors, cosine, sine):
    return vectors * cosine + pltpu.roll(vectors, HEAD_DIM // 2, 1) * sine


def weights_of(query, key, live):
    dots = dot_rt(query, key) * (1.0 / math.sqrt(HEAD_DIM)) - math.log(SEQ_LEN)
    return jax.nn.sigmoid(dots) * live


def attend_kernel(width, rows_ref, w_ref, cos_ref, sin_ref, live_ref, qkv_ref, mixed_ref, part_ref):
    qkv = dot(rows_ref[...], w_ref[:, : 3 * width])
    cosine, sine = cos_ref[...], sin_ref[...]
    live = live_ref[...].astype(f32)
    for first in range(0, width, HEAD_DIM):
        at_q, at_k, at_v = (slice(g + first, g + first + HEAD_DIM) for g in (0, width, 2 * width))
        query = turn(qkv[:, at_q], cosine, sine).astype(low)
        key = turn(qkv[:, at_k], cosine, sine).astype(low)
        value = qkv[:, at_v].astype(low)
        qkv_ref[:, at_q] = query
        qkv_ref[:, at_k] = key
        qkv_ref[:, at_v] = value
        probs = weights_of(query, key, live)
        mixed_ref[:, at_q] = dot(probs.astype(low), value).astype(low)
    part_ref[...] = dot_rt(mixed_ref[...], w_ref[:, 3 * width :]).astype(low)


def attend(rows, weights, cosine, sine, live):
    total, model = rows.shape
    width, seq = weights.shape[1] // 4, live.shape[1]
    tile = lambda columns: pl.BlockSpec((seq, columns), lambda n: (n, 0))
    outs = [jax.ShapeDtypeStruct((total, c), low) for c in (3 * width, width, model)]
    return pl.pallas_call(
        functools.partial(attend_kernel, width),
        grid=(total // seq,),
        in_specs=[tile(model), whole(weights), tile(HEAD_DIM), tile(HEAD_DIM), tile(seq)],
        out_specs=[tile(3 * width), tile(width), tile(model)],
        out_shape=outs,
        compiler_params=params,
        cost_estimate=cost(8 * total * model * width + 4 * total * seq * width, rows, weights, *outs),
    )(rows, weights, cosine, sine, live)


def attend_back_kernel(
    width, grad_ref, w_ref, qkv_ref, cos_ref, sin_ref, live_ref, grads_ref, part_ref
):
    grad_mixed = dot(grad_ref[...], w_ref[:, 3 * width :]).astype(low)
    cosine, sine = cos_ref[...], -sin_ref[...]
    live = live_ref[...].astype(f32)
    scale = 1.0 / math.sqrt(HEAD_DIM)
    for first in range(0, width, HEAD_DIM):
        at_q, at_k, at_v = (slice(g + first, g + first + HEAD_DIM) for g in (0, width, 2 * width))
        query, key, value = qkv_ref[:, at_q], qkv_ref[:, at_k], qkv_ref[:, at_v]
        grad = grad_mixed[:, at_q]
        probs = weights_of(query, key, live)
        grad_dots = (dot_rt(grad, value) * probs * (1.0 - probs)).astype(low)
        grads_ref[:, at_q] = turn(dot(grad_dots, key) * scale, cosine, sine).astype(low)
        grads_ref[:, at_k] = turn(dot_lt(grad_dots, query) * scale, cosine, sine).astype(low)
        grads_ref[:, at_v] = dot_lt(probs.astype(low), grad).astype(low)
    part_ref[...] = dot_rt(grads_ref[...], w_ref[:, : 3 * width]).astype(low)


def attend_back(grad_rows, weights, qkv, cosine, sine, live):
    total, model = grad_rows.shape
    width, seq = weights.shape[1] // 4, live.shape[1]
    tile = lambda columns: pl.BlockSpec((seq, columns), lambda n: (n, 0))
    outs = [jax.ShapeDtypeStruct((total, c), low) for c in (3 * width, model)]
    return pl.pallas_call(
        functools.partial(attend_back_kernel, width),
        grid=(total // seq,),
        in_specs=[
            tile(model),
            whole(weights),
            tile(3 * width),
            tile(HEAD_DIM),
            tile(HEAD_DIM),
            tile(seq),
        ],
        out_specs=[tile(3 * width), tile(model)],
        out_shape=outs,
        compiler_params=params,
        cost_estimate=cost(
            8 * total * model * width + 10 * total * seq * width, grad_rows, weights, qkv, *outs
        ),
    )(grad_rows, weights, qkv, cosine, sine, live)


def gated_kernel(units, rows_ref, grad_ref, w_ref, both_ref, hidden_ref):
    gate = dot(rows_ref[...], w_ref[:, :units])
    upward = dot(rows_ref[...], w_ref[:, units : 2 * units])
    grad_hidden = dot(grad_ref[...], w_ref[:, 2 * units :])
    gate_sig = jax.nn.sigmoid(gate)
    silu = gate * gate_sig
    both_ref[:, :units] = (
        grad_hidden * upward * gate_sig * (1.0 + gate * (1.0 - gate_sig))
    ).astype(low)
    both_ref[:, units:] = (grad_hidden * silu).astype(low)
    hidden_ref[...] = (silu * upward).astype(low)


def gated(rows, grad_rows, weights, tile=512):
    total, model = rows.shape
    units = weights.shape[1] // 3
    tiled = lambda columns: pl.BlockSpec((tile, columns), lambda i: (i, 0))
    outs = [jax.ShapeDtypeStruct((total, c), low) for c in (2 * units, units)]
    return pl.pallas_call(
        functools.partial(gated_kernel, units),
        grid=(total // tile,),
        in_specs=[tiled(model), tiled(model), whole(weights)],
        out_specs=[tiled(2 * units), tiled(units)],
        out_shape=outs,
        compiler_params=params,
        cost_estimate=cost(6 * total * model * units, rows, grad_rows, weights, *outs),
    )(rows, grad_rows, weights)


def project_kernel(first, count, *refs):
    total = None
    for act_ref, w_ref in zip(refs[:count], refs[count : 2 * count]):
        term = dot_rt(act_ref[...], w_ref[:, first : first + act_ref.shape[1]])
        total = term if total is None else total + term
    refs[-1][...] = total.astype(low)


def project(acts, weights, first, tile=256):
    total, wide = acts[0].shape
    model = weights[0].shape[0]
    out = jax.ShapeDtypeStruct((total, model), low)
    return pl.pallas_call(
        functools.partial(project_kernel, first, len(acts)),
        grid=(total // tile,),
        in_specs=[pl.BlockSpec((tile, wide), lambda i: (i, 0))] * len(acts)
        + [whole(w) for w in weights],
        out_specs=pl.BlockSpec((tile, model), lambda i: (i, 0)),
        out_shape=out,
        compiler_params=params,
        cost_estimate=cost(2 * total * model * wide * len(acts), *acts, *weights, out),
    )(*acts, *weights)


def outer_kernel(groups, *refs):
    out_ref = refs[-1]
    refs = list(refs[:-1])
    first = 0
    for count in groups:
        total = None
        for _ in range(count):
            left_ref, right_ref = refs.pop(0), refs.pop(0)
            term = dot_lt(left_ref[...], right_ref[...])
            total = term if total is None else total + term
        out_ref[:, first : first + total.shape[1]] = total.astype(low)
        first += total.shape[1]


def outer(*groups, tile=256):
    model = groups[0][0][0].shape[1]
    wide = sum(group[0][1].shape[1] for group in groups)
    out = jax.ShapeDtypeStruct((model, wide), low)
    operands, specs, flops = [], [], 0
    for group in groups:
        for left, right in group:
            operands += [left, right]
            specs += [pl.BlockSpec((left.shape[0], tile), lambda i: (0, i)), whole(right)]
            flops += 2 * left.shape[0] * model * right.shape[1]
    return pl.pallas_call(
        functools.partial(outer_kernel, [len(group) for group in groups]),
        grid=(model // tile,),
        in_specs=specs,
        out_specs=pl.BlockSpec((tile, wide), lambda i: (i, 0)),
        out_shape=out,
        compiler_params=params,
        cost_estimate=cost(flops, *operands, out),
    )(*operands)


def swap(value, axis):
    return lax.ppermute(value, axis, [(0, 1), (1, 0)])


def gather_first(own):
    half = own.shape[0] // 2
    from_x, from_y = together(swap(own, "tensor"), swap(own, "y"))
    return own, from_x, from_y, (from_x[:half], from_y[half:])


def gather_last(state):
    own, from_x, from_y, (top, bottom) = state
    top, bottom = together(swap(top, "y"), swap(bottom, "tensor"))
    chip = jnp.concatenate([own, from_x, from_y, top, bottom], axis=0)
    return chip, swap(chip, "c")


def scatter_first(mine, theirs):
    rows = mine.shape[0] // 4
    half = rows // 2
    other = swap(theirs, "c")

    def piece(dy, dx, bottom):
        first = (2 * dy + dx) * rows + bottom * half
        return mine[first : first + half].astype(f32) + other[first : first + half].astype(f32)

    top_x = jnp.concatenate([piece(0, 1, 0), piece(1, 1, 0)], axis=0).astype(low)
    bottom_y = jnp.concatenate([piece(1, 0, 1), piece(1, 1, 1)], axis=0).astype(low)
    return piece, half, together(top_x, bottom_y)


def scatter_second(state):
    piece, half, (top_x, bottom_y) = state
    top_x, bottom_y = together(swap(top_x, "tensor"), swap(bottom_y, "y"))
    top_y = (piece(1, 0, 0) + top_x[half:].astype(f32)).astype(low)
    bottom_x = (piece(0, 1, 1) + bottom_y[half:].astype(f32)).astype(low)
    return piece, half, (top_x[:half], bottom_y[:half], top_y, bottom_x)


def scatter_last(state):
    piece, half, (top_x, bottom_y, top_y, bottom_x) = state
    top_y, bottom_x = together(swap(top_y, "y"), swap(bottom_x, "tensor"))
    top = piece(0, 0, 0) + top_x.astype(f32) + top_y.astype(f32)
    bottom = piece(0, 0, 1) + bottom_y.astype(f32) + bottom_x.astype(f32)
    return jnp.concatenate([top, bottom], axis=0)


def beside(state, *others):
    sends, *others = together(state[-1], *others)
    return (*state[:-1], sends), *others


def to_columns(parts):
    block = lax.all_to_all(parts, ("y", "c"), 0, 0, tiled=True)
    return block.reshape(-1, parts.shape[2])


def to_rows(block):
    parts = block.reshape(PLANE, block.shape[0] // PLANE, block.shape[1])
    return lax.all_to_all(parts, ("y", "c"), 0, 0, tiled=True)


def gather_line(block):
    return lax.all_gather(block, "z", axis=0, tiled=True)


def scatter_line(grads):
    return lax.psum_scatter(grads, "z", scatter_dimension=0, tiled=True)


def quarters(weight, width):
    return jnp.swapaxes(weight.reshape(weight.shape[0], PLANE, width), 0, 1)


def shard_of(parts):
    return jnp.swapaxes(parts, 0, 1).reshape(parts.shape[1], -1).astype(f32)


def shifted(value, step):
    count = lax.axis_size("z")
    return lax.ppermute(value, "z", [(i, (i + step) % count) for i in range(count)])


def plane_flip(value, dy, dc):
    if dy and dc:
        return lax.ppermute(value, ("y", "c"), [(i, i ^ 3) for i in range(4)])
    return swap(value, "y" if dy else "c")


def gather_gains(gains, place, level):
    plane = jnp.zeros((PLANE,) + gains.shape, gains.dtype)
    for flip in range(PLANE):
        piece = plane_flip(gains, flip // 2, flip % 2) if flip else gains
        plane = lax.dynamic_update_index_in_dim(plane, piece, place ^ flip, 0)
    count = lax.axis_size("z")
    every = jnp.zeros((count,) + plane.shape, gains.dtype)
    every = lax.dynamic_update_index_in_dim(every, plane, level, 0)
    for step in range(1, count):
        piece = shifted(plane, step)
        every = lax.dynamic_update_index_in_dim(
            every, piece, lax.rem(level - step + count, count), 0
        )
    return jnp.moveaxis(every, 2, 0).reshape(gains.shape[0], -1)


def scatter_gains(part, place, level):
    count = lax.axis_size("z")
    part = part + swap(part, "tensor")
    blocks = part.reshape(part.shape[0], count, PLANE, -1)
    mine = lax.dynamic_index_in_dim(blocks, place, 2, keepdims=False)
    for flip in range(1, PLANE):
        piece = lax.dynamic_index_in_dim(blocks, place ^ flip, 2, keepdims=False)
        mine = mine + plane_flip(piece, flip // 2, flip % 2)
    result = lax.dynamic_index_in_dim(mine, level, 1, keepdims=False)
    for step in range(1, count):
        piece = lax.dynamic_index_in_dim(mine, lax.rem(level + step, count), 1, keepdims=False)
        result = result + shifted(piece, step)
    return result


def normalize(rows):
    scale = lax.rsqrt(jnp.mean(rows * rows, axis=-1, keepdims=True) + epsilon)
    return rows * scale, scale


def norm_back(grad_normed, unit_rows, scale, gain):
    inner = grad_normed * gain
    mean_term = jnp.mean(inner * unit_rows, axis=-1, keepdims=True)
    return scale * (inner - unit_rows * mean_term), jnp.sum(grad_normed * unit_rows, axis=0)


def local(
    tokens,
    segments,
    gain_attn,
    gain_ffn,
    w_query,
    w_key,
    w_value,
    w_out,
    w_gate,
    w_up,
    w_down,
    cotangent,
):
    seq_len = segments.shape[1]
    side = lax.axis_index("tensor")
    level, place = lax.axis_index("z"), lax.axis_index("y") * 2 + lax.axis_index("c")
    width = w_query.shape[1] // PLANE
    units = w_gate.shape[1] // PLANE
    chunk = units // CHUNKS

    attn_block = to_columns(
        jnp.concatenate([quarters(w, width) for w in (w_query, w_key, w_value, w_out)], axis=2)
    )
    wide = [quarters(w, units) for w in (w_gate, w_up, w_down)]
    ffn_parts = [
        jnp.concatenate([w[:, :, k * chunk : (k + 1) * chunk] for w in wide], axis=2)
        for k in range(CHUNKS)
    ]
    ffn_parts[0], attn_block = together(ffn_parts[0], attn_block)
    ffn_first = to_columns(ffn_parts[0])
    attn_weights = gather_line(attn_block)

    gains = gather_gains(jnp.stack([gain_attn, gain_ffn]), place, level)
    seg = jnp.concatenate(
        [segments] + [plane_flip(segments, dy, dc) for dc, dy in ((0, 1), (1, 0), (1, 1))], axis=0
    )
    gains, seg = together(gains, seg)
    gain_first, gain_second = gains[0].astype(f32), gains[1].astype(f32)
    inputs = tokens.astype(f32)
    unit_one, scale_one = normalize(inputs)
    places = lax.rem(jnp.arange(seq_len, dtype=jnp.int32) + side * (seq_len // 2), seq_len)
    seg = jnp.where(side == 0, seg, jnp.roll(seg, seq_len // 2, axis=1))
    same = seg[:, :, None] == seg[:, None, :]
    live = same & (places[None, None, :] <= places[None, :, None])
    positions = jnp.sum(live.astype(jnp.int32), axis=2) - 1
    freqs = theta ** (-(jnp.arange(HEAD_DIM // 2, dtype=f32) * 2.0 / HEAD_DIM))
    angles = (positions.astype(f32)[..., None] * freqs).reshape(2, -1, HEAD_DIM // 2)
    cosine, sine = jnp.cos(angles), jnp.sin(angles)
    cosine = jnp.concatenate([cosine, cosine], axis=2)
    sine = jnp.concatenate([-sine, sine], axis=2)
    live = live.astype(low).reshape(2, -1, seq_len)
    sides = range(2)
    state, live, cosine, sine, ffn_first = beside(
        gather_first((unit_one * gain_first).astype(low)), live, cosine, sine, ffn_first
    )
    rows_one = gather_last(state)
    ffn_weights = [gather_line(ffn_first)]
    ffn_parts[1], rows_own = together(ffn_parts[1], rows_one[0])
    rows_one = (rows_own, rows_one[1])
    ffn_second = to_columns(ffn_parts[1])
    grad_own, attn_weights, ffn_second = together(cotangent, attn_weights, ffn_second)
    ffn_weights.append(gather_line(ffn_second))

    qkv, mixed, parts = zip(
        *(attend(rows_one[i], attn_weights, cosine[i], sine[i], live[i]) for i in sides)
    )
    grad_state, parts = beside(gather_first(grad_own), parts)
    middle = inputs + scatter_last(scatter_second(scatter_first(*parts)))
    unit_two, scale_two = normalize(middle)
    rows_two = gather_last(gather_first((unit_two * gain_second).astype(low)))
    grad_state, rows_own = beside(grad_state, rows_two[0])
    rows_two = (rows_own, rows_two[1])
    grad_rows = gather_last(grad_state)

    both = [[None] * CHUNKS for _ in sides]
    hidden = [[None] * CHUNKS for _ in sides]
    ffn_sums = []
    grad_parts = None
    for k in range(CHUNKS):
        for i in sides:
            both[i][k], hidden[i][k] = gated(rows_two[i], grad_rows[i], ffn_weights[k])
        if k == CHUNKS - 1:
            grad_parts = [project(both[i], ffn_weights, 0) for i in sides]
        sums = outer(
            [(rows_two[i], both[i][k]) for i in sides],
            [(grad_rows[i], hidden[i][k]) for i in sides],
        )
        if k == CHUNKS - 1:
            grad_state, sums = beside(scatter_second(scatter_first(*grad_parts)), sums)
        ffn_sums.append(scatter_line(sums))
    grad_normed_two = scatter_last(grad_state)
    grad_unit_two, gain_two_part = norm_back(grad_normed_two, unit_two, scale_two, gain_second)
    grad_middle = cotangent.astype(f32) + grad_unit_two
    grad_branch = gather_first(grad_middle.astype(low))
    out_parts = [project(hidden[i], ffn_weights, 2 * chunk) for i in sides]
    grad_branch, out_parts = beside(grad_branch, out_parts)
    grad_branch = gather_last(grad_branch)
    out_state, grad_own = beside(scatter_first(*out_parts), grad_branch[0])
    grad_branch = (grad_own, grad_branch[1])

    grads, parts = zip(
        *(
            attend_back(grad_branch[i], attn_weights, qkv[i], cosine[i], sine[i], live[i])
            for i in sides
        )
    )
    ffn_rows = [to_rows(ffn_sums[0])]
    out_state, grads, ffn_rows = beside(scatter_second(out_state), grads, ffn_rows)
    sums = outer(
        [(rows_one[i], grads[i]) for i in sides],
        [(grad_branch[i], mixed[i]) for i in sides],
    )
    sums, out_sums = together(sums, scatter_last(out_state))
    attn_sums = to_rows(scatter_line(sums))
    output = (middle + out_sums).astype(low)
    grad_normed_one = scatter_last(scatter_second(scatter_first(*parts)))
    ffn_rows += [to_rows(s) for s in ffn_sums[1:]]
    grad_unit_one, gain_one_part = norm_back(grad_normed_one, unit_one, scale_one, gain_first)
    grad_tokens = grad_middle + grad_unit_one
    gain_sums = scatter_gains(jnp.stack([gain_one_part, gain_two_part]), place, level)

    attn_grads = [shard_of(attn_sums[:, :, k * width : (k + 1) * width]) for k in range(4)]
    ffn_grads = [
        shard_of(jnp.concatenate([s[:, :, k * chunk : (k + 1) * chunk] for s in ffn_rows], axis=2))
        for k in range(3)
    ]
    return (output, grad_tokens, gain_sums[0], gain_sums[1], *attn_grads, *ffn_grads)


def solution(mesh):
    lines = mesh.shape["dp"] // PLANE
    finer = Mesh(
        mesh.devices.reshape(lines, 2, 2, mesh.shape["tensor"]), ("z", "y", "c", "tensor")
    )
    dp = ("z", "y", "c")
    rows, grid = P(dp + ("tensor",), None), P(dp, "tensor")
    return jax.shard_map(
        local,
        mesh=finer,
        in_specs=(rows, P(dp, None), P(dp), P(dp)) + (grid,) * 7 + (rows,),
        out_specs=(rows, rows, P(dp), P(dp)) + (grid,) * 7,
        check_vma=False,
    )
```

```python
import functools
import math

import jax
import jax.numpy as jnp
from jax import lax
from jax.experimental import pallas as pl
from jax.experimental.pallas import tpu as pltpu
from jax.sharding import Mesh
from jax.sharding import PartitionSpec as P

HEAD_DIM = 128
SEQ_LEN = 512
PLANE = 4
CHUNKS = 2

epsilon = 1e-05
theta = 10000.0
low = jnp.bfloat16
f32 = jnp.float32
params = pltpu.CompilerParams(vmem_limit_bytes=56 * 2**20)


def dot(left, right):
    return jnp.dot(left, right, preferred_element_type=f32)


def dot_rt(left, right):
    return lax.dot_general(left, right, (((1,), (1,)), ((), ())), preferred_element_type=f32)


def dot_lt(left, right):
    return lax.dot_general(left, right, (((0,), (0,)), ((), ())), preferred_element_type=f32)


def after(value, *earlier):
    return lax.optimization_barrier((value,) + earlier)[0]


def together(*values):
    return lax.optimization_barrier(values)


def whole(array):
    return pl.BlockSpec(array.shape, lambda i: (0,) * array.ndim)


def cost(flops, *arrays):
    size = sum(math.prod(a.shape) * a.dtype.itemsize for a in arrays)
    return pl.CostEstimate(flops=flops, bytes_accessed=size, transcendentals=0)


def turn(vectors, cosine, sine):
    return vectors * cosine + pltpu.roll(vectors, HEAD_DIM // 2, 1) * sine


def weights_of(query, key, live):
    dots = dot_rt(query, key) * (1.0 / math.sqrt(HEAD_DIM)) - math.log(SEQ_LEN)
    return jax.nn.sigmoid(dots) * live


def attend_kernel(width, rows_ref, w_ref, cos_ref, sin_ref, live_ref, qkv_ref, mixed_ref, part_ref):
    qkv = dot(rows_ref[...], w_ref[:, : 3 * width])
    cosine, sine = cos_ref[...], sin_ref[...]
    live = live_ref[...].astype(f32)
    for first in range(0, width, HEAD_DIM):
        at_q, at_k, at_v = (slice(g + first, g + first + HEAD_DIM) for g in (0, width, 2 * width))
        query = turn(qkv[:, at_q], cosine, sine).astype(low)
        key = turn(qkv[:, at_k], cosine, sine).astype(low)
        value = qkv[:, at_v].astype(low)
        qkv_ref[:, at_q] = query
        qkv_ref[:, at_k] = key
        qkv_ref[:, at_v] = value
        probs = weights_of(query, key, live)
        mixed_ref[:, at_q] = dot(probs.astype(low), value).astype(low)
    part_ref[...] = dot_rt(mixed_ref[...], w_ref[:, 3 * width :]).astype(low)


def attend(rows, weights, cosine, sine, live):
    total, model = rows.shape
    width, seq = weights.shape[1] // 4, live.shape[1]
    tile = lambda columns: pl.BlockSpec((seq, columns), lambda n: (n, 0))
    outs = [jax.ShapeDtypeStruct((total, c), low) for c in (3 * width, width, model)]
    return pl.pallas_call(
        functools.partial(attend_kernel, width),
        grid=(total // seq,),
        in_specs=[tile(model), whole(weights), tile(HEAD_DIM), tile(HEAD_DIM), tile(seq)],
        out_specs=[tile(3 * width), tile(width), tile(model)],
        out_shape=outs,
        compiler_params=params,
        cost_estimate=cost(8 * total * model * width + 4 * total * seq * width, rows, weights, *outs),
    )(rows, weights, cosine, sine, live)


def attend_back_kernel(
    width, grad_ref, w_ref, qkv_ref, cos_ref, sin_ref, live_ref, grads_ref, part_ref
):
    grad_mixed = dot(grad_ref[...], w_ref[:, 3 * width :]).astype(low)
    cosine, sine = cos_ref[...], -sin_ref[...]
    live = live_ref[...].astype(f32)
    scale = 1.0 / math.sqrt(HEAD_DIM)
    for first in range(0, width, HEAD_DIM):
        at_q, at_k, at_v = (slice(g + first, g + first + HEAD_DIM) for g in (0, width, 2 * width))
        query, key, value = qkv_ref[:, at_q], qkv_ref[:, at_k], qkv_ref[:, at_v]
        grad = grad_mixed[:, at_q]
        probs = weights_of(query, key, live)
        grad_dots = (dot_rt(grad, value) * probs * (1.0 - probs)).astype(low)
        grads_ref[:, at_q] = turn(dot(grad_dots, key) * scale, cosine, sine).astype(low)
        grads_ref[:, at_k] = turn(dot_lt(grad_dots, query) * scale, cosine, sine).astype(low)
        grads_ref[:, at_v] = dot_lt(probs.astype(low), grad).astype(low)
    part_ref[...] = dot_rt(grads_ref[...], w_ref[:, : 3 * width]).astype(low)


def attend_back(grad_rows, weights, qkv, cosine, sine, live):
    total, model = grad_rows.shape
    width, seq = weights.shape[1] // 4, live.shape[1]
    tile = lambda columns: pl.BlockSpec((seq, columns), lambda n: (n, 0))
    outs = [jax.ShapeDtypeStruct((total, c), low) for c in (3 * width, model)]
    return pl.pallas_call(
        functools.partial(attend_back_kernel, width),
        grid=(total // seq,),
        in_specs=[
            tile(model),
            whole(weights),
            tile(3 * width),
            tile(HEAD_DIM),
            tile(HEAD_DIM),
            tile(seq),
        ],
        out_specs=[tile(3 * width), tile(model)],
        out_shape=outs,
        compiler_params=params,
        cost_estimate=cost(
            8 * total * model * width + 10 * total * seq * width, grad_rows, weights, qkv, *outs
        ),
    )(grad_rows, weights, qkv, cosine, sine, live)


def gated_kernel(units, rows_ref, grad_ref, w_ref, both_ref, hidden_ref):
    gate = dot(rows_ref[...], w_ref[:, :units])
    upward = dot(rows_ref[...], w_ref[:, units : 2 * units])
    grad_hidden = dot(grad_ref[...], w_ref[:, 2 * units :])
    gate_sig = jax.nn.sigmoid(gate)
    silu = gate * gate_sig
    both_ref[:, :units] = (
        grad_hidden * upward * gate_sig * (1.0 + gate * (1.0 - gate_sig))
    ).astype(low)
    both_ref[:, units:] = (grad_hidden * silu).astype(low)
    hidden_ref[...] = (silu * upward).astype(low)


def gated(rows, grad_rows, weights, tile=512):
    total, model = rows.shape
    units = weights.shape[1] // 3
    tiled = lambda columns: pl.BlockSpec((tile, columns), lambda i: (i, 0))
    outs = [jax.ShapeDtypeStruct((total, c), low) for c in (2 * units, units)]
    return pl.pallas_call(
        functools.partial(gated_kernel, units),
        grid=(total // tile,),
        in_specs=[tiled(model), tiled(model), whole(weights)],
        out_specs=[tiled(2 * units), tiled(units)],
        out_shape=outs,
        compiler_params=params,
        cost_estimate=cost(6 * total * model * units, rows, grad_rows, weights, *outs),
    )(rows, grad_rows, weights)


def project_kernel(first, count, *refs):
    total = None
    for act_ref, w_ref in zip(refs[:count], refs[count : 2 * count]):
        term = dot_rt(act_ref[...], w_ref[:, first : first + act_ref.shape[1]])
        total = term if total is None else total + term
    for ref in refs[2 * count : -1]:
        total = total + ref[...]
    refs[-1][...] = total.astype(refs[-1].dtype)


def project(acts, weights, first, *earlier, dtype=low, tile=256):
    total, wide = acts[0].shape
    model = weights[0].shape[0]
    out = jax.ShapeDtypeStruct((total, model), dtype)
    tiled = lambda columns: pl.BlockSpec((tile, columns), lambda i: (i, 0))
    return pl.pallas_call(
        functools.partial(project_kernel, first, len(acts)),
        grid=(total // tile,),
        in_specs=[tiled(wide)] * len(acts)
        + [whole(w) for w in weights]
        + [tiled(model)] * len(earlier),
        out_specs=tiled(model),
        out_shape=out,
        compiler_params=params,
        cost_estimate=cost(
            2 * total * model * wide * len(acts), *acts, *weights, *earlier, out
        ),
    )(*acts, *weights, *earlier)


def outer_kernel(groups, *refs):
    out_ref = refs[-1]
    refs = list(refs[:-1])
    first = 0
    for count in groups:
        total = None
        for _ in range(count):
            left_ref, right_ref = refs.pop(0), refs.pop(0)
            term = dot_lt(left_ref[...], right_ref[...])
            total = term if total is None else total + term
        out_ref[:, first : first + total.shape[1]] = total.astype(low)
        first += total.shape[1]


def outer(*groups, tile=256):
    model = groups[0][0][0].shape[1]
    wide = sum(group[0][1].shape[1] for group in groups)
    out = jax.ShapeDtypeStruct((model, wide), low)
    operands, specs, flops = [], [], 0
    for group in groups:
        for left, right in group:
            operands += [left, right]
            specs += [pl.BlockSpec((left.shape[0], tile), lambda i: (0, i)), whole(right)]
            flops += 2 * left.shape[0] * model * right.shape[1]
    return pl.pallas_call(
        functools.partial(outer_kernel, [len(group) for group in groups]),
        grid=(model // tile,),
        in_specs=specs,
        out_specs=pl.BlockSpec((tile, wide), lambda i: (i, 0)),
        out_shape=out,
        compiler_params=params,
        cost_estimate=cost(flops, *operands, out),
    )(*operands)


def pack_kernel(width, *refs):
    out_ref = refs[-1]
    for k, ref in enumerate(refs[:-1]):
        for q in range(PLANE):
            out_ref[q, :, k * width : (k + 1) * width] = ref[:, q * width : (q + 1) * width]


def pack(*weights):
    rows, columns = weights[0].shape
    width = columns // PLANE
    out = jax.ShapeDtypeStruct((PLANE, rows, width * len(weights)), low)
    return pl.pallas_call(
        functools.partial(pack_kernel, width),
        out_shape=out,
        compiler_params=params,
        cost_estimate=cost(0, *weights, out),
    )(*weights)


def unpack_kernel(width, parts_ref, *out_refs):
    for k, ref in enumerate(out_refs):
        for q in range(PLANE):
            ref[:, q * width : (q + 1) * width] = parts_ref[
                q, :, k * width : (k + 1) * width
            ].astype(f32)


def unpack(parts, count):
    rows, width = parts.shape[1], parts.shape[2] // count
    outs = [jax.ShapeDtypeStruct((rows, PLANE * width), f32)] * count
    return pl.pallas_call(
        functools.partial(unpack_kernel, width),
        out_shape=outs,
        compiler_params=params,
        cost_estimate=cost(0, parts, *outs),
    )(parts)


def swap(value, axis):
    return lax.ppermute(value, axis, [(0, 1), (1, 0)])


def gather_first(own):
    half = own.shape[0] // 2
    from_x, from_y = together(swap(own, "tensor"), swap(own, "y"))
    return own, from_x, from_y, (from_x[:half], from_y[half:])


def gather_last(state, *before_core):
    own, from_x, from_y, (top, bottom) = state
    top, bottom = together(swap(top, "y"), swap(bottom, "tensor"))
    chip = jnp.concatenate([own, from_x, from_y, top, bottom], axis=0)
    if before_core:
        chip, *before_core = together(chip, *before_core)
    return chip, swap(chip, "c"), *before_core


def scatter_first(mine, theirs):
    rows = mine.shape[0] // 4
    half = rows // 2
    other = swap(theirs, "c")

    def piece(dy, dx, bottom):
        first = (2 * dy + dx) * rows + bottom * half
        return mine[first : first + half].astype(f32) + other[first : first + half].astype(f32)

    top_x = jnp.concatenate([piece(0, 1, 0), piece(1, 1, 0)], axis=0).astype(low)
    bottom_y = jnp.concatenate([piece(1, 0, 1), piece(1, 1, 1)], axis=0).astype(low)
    return piece, half, together(top_x, bottom_y)


def scatter_second(state):
    piece, half, (top_x, bottom_y) = state
    top_x, bottom_y = together(swap(top_x, "tensor"), swap(bottom_y, "y"))
    top_y = (piece(1, 0, 0) + top_x[half:].astype(f32)).astype(low)
    bottom_x = (piece(0, 1, 1) + bottom_y[half:].astype(f32)).astype(low)
    return piece, half, (top_x[:half], bottom_y[:half], top_y, bottom_x)


def scatter_last(state):
    piece, half, (top_x, bottom_y, top_y, bottom_x) = state
    top_y, bottom_x = together(swap(top_y, "y"), swap(bottom_x, "tensor"))
    top = piece(0, 0, 0) + top_x.astype(f32) + top_y.astype(f32)
    bottom = piece(0, 0, 1) + bottom_y.astype(f32) + bottom_x.astype(f32)
    return jnp.concatenate([top, bottom], axis=0)


def beside(state, *others):
    sends, *others = together(state[-1], *others)
    return (*state[:-1], sends), *others


def to_columns(parts):
    block = lax.all_to_all(parts, ("y", "c"), 0, 0, tiled=True)
    return block.reshape(-1, parts.shape[2])


def to_rows(block):
    parts = block.reshape(PLANE, block.shape[0] // PLANE, block.shape[1])
    return lax.all_to_all(parts, ("y", "c"), 0, 0, tiled=True)


def gather_line(block):
    return lax.all_gather(block, "z", axis=0, tiled=True)


def scatter_line(grads):
    return lax.psum_scatter(grads, "z", scatter_dimension=0, tiled=True)


def quarters(weight, width):
    return jnp.swapaxes(weight.reshape(weight.shape[0], PLANE, width), 0, 1)


def shard_of(parts):
    return jnp.swapaxes(parts, 0, 1).reshape(parts.shape[1], -1).astype(f32)


def shifted(value, step):
    count = lax.axis_size("z")
    return lax.ppermute(value, "z", [(i, (i + step) % count) for i in range(count)])


def plane_flip(value, dy, dc):
    if dy and dc:
        return lax.ppermute(value, ("y", "c"), [(i, i ^ 3) for i in range(4)])
    return swap(value, "y" if dy else "c")


def gather_gains(gains, place, level):
    plane = jnp.zeros((PLANE,) + gains.shape, gains.dtype)
    for flip in range(PLANE):
        piece = plane_flip(gains, flip // 2, flip % 2) if flip else gains
        plane = lax.dynamic_update_index_in_dim(plane, piece, place ^ flip, 0)
    count = lax.axis_size("z")
    every = jnp.zeros((count,) + plane.shape, gains.dtype)
    every = lax.dynamic_update_index_in_dim(every, plane, level, 0)
    for step in range(1, count):
        piece = shifted(plane, step)
        every = lax.dynamic_update_index_in_dim(
            every, piece, lax.rem(level - step + count, count), 0
        )
    return jnp.moveaxis(every, 2, 0).reshape(gains.shape[0], -1)


def scatter_gains(part, place, level):
    count = lax.axis_size("z")
    part = part + swap(part, "tensor")
    blocks = part.reshape(part.shape[0], count, PLANE, -1)
    mine = lax.dynamic_index_in_dim(blocks, place, 2, keepdims=False)
    for flip in range(1, PLANE):
        piece = lax.dynamic_index_in_dim(blocks, place ^ flip, 2, keepdims=False)
        mine = mine + plane_flip(piece, flip // 2, flip % 2)
    result = lax.dynamic_index_in_dim(mine, level, 1, keepdims=False)
    for step in range(1, count):
        piece = lax.dynamic_index_in_dim(mine, lax.rem(level + step, count), 1, keepdims=False)
        result = result + shifted(piece, step)
    return result


def normalize(rows):
    scale = lax.rsqrt(jnp.mean(rows * rows, axis=-1, keepdims=True) + epsilon)
    return rows * scale, scale


def norm_back(grad_normed, unit_rows, scale, gain):
    inner = grad_normed * gain
    mean_term = jnp.mean(inner * unit_rows, axis=-1, keepdims=True)
    return scale * (inner - unit_rows * mean_term), jnp.sum(grad_normed * unit_rows, axis=0)


def local(
    tokens,
    segments,
    gain_attn,
    gain_ffn,
    w_query,
    w_key,
    w_value,
    w_out,
    w_gate,
    w_up,
    w_down,
    cotangent,
):
    seq_len = segments.shape[1]
    side = lax.axis_index("tensor")
    level, place = lax.axis_index("z"), lax.axis_index("y") * 2 + lax.axis_index("c")
    width = w_query.shape[1] // PLANE
    units = w_gate.shape[1] // PLANE
    chunk = units // CHUNKS

    attn_parts = pack(w_query, w_key, w_value, w_out)
    attn_parts, gain_attn, gain_ffn, segments = together(
        attn_parts, gain_attn, gain_ffn, segments
    )
    attn_block = to_columns(attn_parts)
    wide = [quarters(w, units) for w in (w_gate, w_up, w_down)]
    ffn_parts = [
        jnp.concatenate([w[:, :, k * chunk : (k + 1) * chunk] for w in wide], axis=2)
        for k in range(CHUNKS)
    ]
    ffn_parts[0], attn_block = together(ffn_parts[0], attn_block)
    ffn_first = to_columns(ffn_parts[0])
    attn_weights = gather_line(attn_block)

    gains = gather_gains(jnp.stack([gain_attn, gain_ffn]), place, level)
    seg = jnp.concatenate(
        [segments] + [plane_flip(segments, dy, dc) for dc, dy in ((0, 1), (1, 0), (1, 1))], axis=0
    )
    gains, seg = together(gains, seg)
    gain_first, gain_second = gains[0].astype(f32), gains[1].astype(f32)
    inputs = tokens.astype(f32)
    unit_one, scale_one = normalize(inputs)
    places = lax.rem(jnp.arange(seq_len, dtype=jnp.int32) + side * (seq_len // 2), seq_len)
    seg = jnp.where(side == 0, seg, jnp.roll(seg, seq_len // 2, axis=1))
    same = seg[:, :, None] == seg[:, None, :]
    live = same & (places[None, None, :] <= places[None, :, None])
    positions = jnp.sum(live.astype(jnp.int32), axis=2) - 1
    freqs = theta ** (-(jnp.arange(HEAD_DIM // 2, dtype=f32) * 2.0 / HEAD_DIM))
    angles = (positions.astype(f32)[..., None] * freqs).reshape(2, -1, HEAD_DIM // 2)
    cosine, sine = jnp.cos(angles), jnp.sin(angles)
    cosine = jnp.concatenate([cosine, cosine], axis=2)
    sine = jnp.concatenate([-sine, sine], axis=2)
    live = live.astype(low).reshape(2, -1, seq_len)
    sides = range(2)
    state, live, cosine, sine, ffn_first = beside(
        gather_first((unit_one * gain_first).astype(low)), live, cosine, sine, ffn_first
    )
    *rows_one, attn_weights = gather_last(state, attn_weights)
    ffn_weights = [gather_line(ffn_first)]
    grad_own, attn_weights = together(cotangent, attn_weights)

    qkv, mixed, parts = [None, None], [None, None], [None, None]
    for i in sides:
        qkv[i], mixed[i], parts[i] = attend(rows_one[i], attn_weights, cosine[i], sine[i], live[i])
    parts[0], ffn_parts[1] = together(parts[0], ffn_parts[1])
    ffn_second = to_columns(ffn_parts[1])
    grad_state, parts = beside(gather_first(grad_own), parts)
    state, ffn_second = beside(scatter_second(scatter_first(*parts)), ffn_second)
    ffn_weights.append(gather_line(ffn_second))
    middle = inputs + scatter_last(state)
    unit_two, scale_two = normalize(middle)
    rows_two = gather_last(gather_first((unit_two * gain_second).astype(low)))
    grad_state, rows_own = beside(grad_state, rows_two[0])
    rows_two = (rows_own, rows_two[1])
    grad_rows = gather_last(grad_state)

    both = [[None] * CHUNKS for _ in sides]
    hidden = [[None] * CHUNKS for _ in sides]
    ffn_sums = []
    grad_parts = None
    for k in range(CHUNKS):
        for i in sides:
            both[i][k], hidden[i][k] = gated(rows_two[i], grad_rows[i], ffn_weights[k])
        if k == CHUNKS - 1:
            grad_parts = [
                project(both[i][k:], ffn_weights[k:], 0, grad_parts[i]) for i in sides
            ]
        sums = outer(
            [(rows_two[i], both[i][k]) for i in sides],
            [(grad_rows[i], hidden[i][k]) for i in sides],
        )
        if k < CHUNKS - 1:
            grad_parts = [
                project([both[i][k]], [ffn_weights[k]], 0, dtype=f32) for i in sides
            ]
            grad_parts, ffn_weights[k + 1] = together(grad_parts, ffn_weights[k + 1])
        if k == CHUNKS - 1:
            grad_state, sums = beside(scatter_second(scatter_first(*grad_parts)), sums)
        ffn_sums.append(scatter_line(sums))
    grad_normed_two = scatter_last(grad_state)
    grad_unit_two, gain_two_part = norm_back(grad_normed_two, unit_two, scale_two, gain_second)
    grad_middle = cotangent.astype(f32) + grad_unit_two
    grad_branch = gather_first(grad_middle.astype(low))
    out_parts = [project(hidden[i], ffn_weights, 2 * chunk) for i in sides]
    grad_branch, out_parts = beside(grad_branch, out_parts)
    grad_branch = gather_last(grad_branch)
    out_state, grad_own = beside(scatter_first(*out_parts), grad_branch[0])
    grad_branch = (grad_own, grad_branch[1])

    grads, parts = zip(
        *(
            attend_back(grad_branch[i], attn_weights, qkv[i], cosine[i], sine[i], live[i])
            for i in sides
        )
    )
    ffn_rows = [to_rows(ffn_sums[0])]
    out_state, grads, ffn_rows = beside(scatter_second(out_state), grads, ffn_rows)
    sums = outer(
        [(rows_one[i], grads[i]) for i in sides],
        [(grad_branch[i], mixed[i]) for i in sides],
    )
    sums, out_sums = together(sums, scatter_last(out_state))
    attn_sums = to_rows(scatter_line(sums))
    output = (middle + out_sums).astype(low)
    grad_normed_one = scatter_last(scatter_second(scatter_first(*parts)))
    ffn_rows += [to_rows(s) for s in ffn_sums[1:]]
    grad_unit_one, gain_one_part = norm_back(grad_normed_one, unit_one, scale_one, gain_first)
    grad_tokens = grad_middle + grad_unit_one
    gain_sums = scatter_gains(jnp.stack([gain_one_part, gain_two_part]), place, level)

    attn_grads = [shard_of(attn_sums[:, :, k * width : (k + 1) * width]) for k in range(4)]
    ffn_grads = [
        shard_of(jnp.concatenate([s[:, :, k * chunk : (k + 1) * chunk] for s in ffn_rows], axis=2))
        for k in range(3)
    ]
    return (output, grad_tokens, gain_sums[0], gain_sums[1], *attn_grads, *ffn_grads)


def solution(mesh):
    lines = mesh.shape["dp"] // PLANE
    finer = Mesh(
        mesh.devices.reshape(lines, 2, 2, mesh.shape["tensor"]), ("z", "y", "c", "tensor")
    )
    dp = ("z", "y", "c")
    rows, grid = P(dp + ("tensor",), None), P(dp, "tensor")
    return jax.shard_map(
        local,
        mesh=finer,
        in_specs=(rows, P(dp, None), P(dp), P(dp)) + (grid,) * 7 + (rows,),
        out_specs=(rows, rows, P(dp), P(dp)) + (grid,) * 7,
        check_vma=False,
    )
```
